32 devices in a mesh: row: 8 (over y, x, core), col: 4 (over z).
Axes of the slice: x: 2, y: 2, z: 4, core: 2. Of those that a mesh axis runs over, the one named last changes fastest.
Arguments:
- click_tiles: bfloat16 [256, 512, 512], P(('row', 'col')), may hold values from 0 to 20
- tile_coords: int32 [256, 2], P(('row', 'col')), may hold values from 0 to 7, as said below
- tile_count: int32 [32], P(('row', 'col')), may hold values from 1 to 8, as said below
- prior_labels: float32 [64, 16384], P(None, ('row', 'col')), may hold values from 0.01 to 10
- seed_ids: int32 [1024], P(('row', 'col')), may hold values from 0 to 16383, as said below
- seed_class: int32 [1024], P(('row', 'col')), may hold values from 0 to 63
Outputs:
- query_labels: float32 [64, 16384], P(None, ('row', 'col'))
- url_labels: float32 [64, 16384], P(None, ('col', 'row'))
The draws below stay inside these ranges and needn't reach their ends.
Inputs may be any that keep to these rules, and one draw needn't show every extreme that they name: `tile_coords`: within each device's 8 slots the (local query block, local URL block) pairs are distinct, first column below 4, second below 8. `tile_count`: some device has all 8 slots live. `seed_ids`: seeds d * 32 to (d + 1) * 32 - 1 name queries d * 512 to (d + 1) * 512 - 1.
All inputs are finite; a program needn't handle non-finite values.
Results may differ from the reference program's by a relative error of at most 0.00097.
Values may be sent and summed in bfloat16 or wider, within the bound.
A program may use at most 64 MiB of HBM per device.

```python
import math
import jax
import jax.numpy as jnp
from jax import lax

CLASSES = 64
TILE = 512
BR = 4
BC = 8
KT = 8
SEED_DEV = 32
ITERS = 2
QDEV = 512
QUERIES = 16384
URLS = 16384
TILES = 256
SEEDS = 1024
N_COL = 4
DEVICES = 32


def draw_tile_coords(key, part):
    key = jax.random.fold_in(key, 1)
    keys = jax.random.split(key, DEVICES)
    orders = jax.vmap(lambda k: jax.random.permutation(k, BR * BC))(keys)[:, :KT]
    places = orders.reshape(TILES).astype(jnp.int32)
    return jnp.stack([places // BC, places % BC], axis=1).astype(jnp.int32)


def draw_tile_count(key, part):
    key = jax.random.fold_in(key, 2)
    first, second, third = jax.random.split(key, 3)
    upper = jax.random.randint(first, (DEVICES,), 1, KT + 1)
    lower = jax.random.randint(second, (DEVICES,), 1, KT + 1)
    counts = jnp.minimum(upper, lower)
    chosen = jax.random.randint(third, (), 0, DEVICES)
    return counts.at[chosen].set(KT).astype(jnp.int32)


def draw_seed_ids(key, part):
    key = jax.random.fold_in(key, 3)
    offsets = jnp.repeat(jnp.arange(DEVICES, dtype=jnp.int32) * QDEV, SEED_DEV)
    inside = jax.random.randint(key, (SEEDS,), 0, QDEV)
    values = offsets + inside
    values = values.at[0].set(0).at[SEEDS - 1].set(QUERIES - 1)
    return values.astype(jnp.int32)


def draw_click_tiles(key, part):
    key = jax.random.fold_in(key, 4)
    pick_key, size_key = jax.random.split(key, 2)
    shape = (TILES, TILE, TILE)
    present = jax.random.randint(pick_key, shape, 0, 16) == 0
    level = 1.0 - jax.random.uniform(size_key, shape, jnp.float32)
    values = 0.05 * jnp.exp(-jnp.log(level) / 1.2)
    values = jnp.minimum(values, 20.0)
    return jnp.where(present, values, 0.0).astype(jnp.bfloat16)


def draw_prior_labels(key, part):
    key = jax.random.fold_in(key, 5)
    first_key, second_key, both_key, base_key, peak_key = jax.random.split(key, 5)
    first = jax.random.randint(first_key, (QUERIES,), 0, CLASSES)
    second = (first + jax.random.randint(second_key, (QUERIES,), 1, CLASSES)) % CLASSES
    has_second = jax.random.randint(both_key, (QUERIES,), 0, 2).astype(jnp.float32)
    class_index = jnp.arange(CLASSES, dtype=jnp.int32)[:, None]
    base = jnp.exp(jax.random.uniform(base_key, (CLASSES, QUERIES), jnp.float32, math.log(0.01), math.log(0.1)))
    peaks = jnp.exp(jax.random.uniform(peak_key, (2, QUERIES), jnp.float32, 0.0, math.log(9.9)))
    first_part = peaks[0][None, :] * (class_index == first[None, :]).astype(jnp.float32)
    second_part = (peaks[1] * has_second)[None, :] * (class_index == second[None, :]).astype(jnp.float32)
    return (base + first_part + second_part).astype(jnp.float32)


def plant(result, own_key, least, high):
    shape = result.shape
    spot = [jax.random.randint(jax.random.fold_in(own_key, axis), (), 0, shape[axis]) for axis in range(len(shape))]
    result = result.at[tuple(spot)].set(least)
    longest = shape.index(max(shape))
    spot[longest] = (spot[longest] + 1) % shape[longest]
    return result.at[tuple(spot)].set(high)


def setup_inputs(seed: int = 0) -> dict:
    arg_keys = jax.random.split(jax.random.key(seed), 7)
    return {
        "click_tiles": draw_click_tiles(jax.random.fold_in(arg_keys[6], 71), 0),
        "tile_coords": draw_tile_coords(jax.random.fold_in(arg_keys[6], 71), 0),
        "tile_count": draw_tile_count(jax.random.fold_in(arg_keys[6], 71), 0),
        "prior_labels": draw_prior_labels(jax.random.fold_in(arg_keys[6], 71), 0),
        "seed_ids": draw_seed_ids(jax.random.fold_in(arg_keys[6], 71), 0),
        "seed_class": plant(jax.random.randint(arg_keys[5], (SEEDS,), 0, CLASSES), jax.random.fold_in(arg_keys[5], 1), 0, CLASSES - 1).astype(jnp.int32),
    }


blend_rate = 0.25
seed_weight = 8.0


def reference(click_tiles, tile_coords, tile_count, prior_labels, seed_ids, seed_class):
    queries = prior_labels.shape[1]
    query_blocks = queries // TILE
    url_blocks = URLS // TILE
    positions = jnp.arange(TILES, dtype=jnp.int32)
    device = positions // KT
    within = positions % KT
    active = (within < tile_count[device]).astype(jnp.float32)
    global_rows = ((device // N_COL) * BR + tile_coords[:, 0]).astype(jnp.int32)
    global_cols = ((device % N_COL) * BC + tile_coords[:, 1]).astype(jnp.int32)
    items = (click_tiles, global_rows, global_cols, active)

    def degree_step(carry, item):
        block, qrow, ucol, weight = item
        query_deg, url_deg = carry
        wide = block.astype(jnp.float32)
        query_deg = query_deg.at[qrow].add(weight * jnp.sum(wide, axis=1))
        url_deg = url_deg.at[ucol].add(weight * jnp.sum(wide, axis=0))
        return (query_deg, url_deg), None

    zero_q = jnp.zeros((query_blocks, TILE), jnp.float32)
    zero_u = jnp.zeros((url_blocks, TILE), jnp.float32)
    (query_deg, url_deg), _ = lax.scan(degree_step, (zero_q, zero_u), items)
    query_deg = query_deg.reshape(queries)
    url_deg = url_deg.reshape(URLS)
    seed_map = jnp.zeros((CLASSES, queries), jnp.float32).at[seed_class, seed_ids].add(1.0)

    labels = prior_labels
    url_labels = jnp.zeros((CLASSES, URLS), jnp.float32)
    for iteration in range(ITERS):
        query_rounded = labels.astype(jnp.bfloat16).reshape(CLASSES, query_blocks, TILE)

        def url_step(carry, item):
            block, qrow, ucol, weight = item
            piece = query_rounded[:, qrow, :]
            term = jnp.dot(piece, block, preferred_element_type=jnp.float32)
            return carry.at[:, ucol, :].add(weight * term), None

        url_sums, _ = lax.scan(url_step, jnp.zeros((CLASSES, url_blocks, TILE), jnp.float32), items)
        url_labels = url_sums.reshape(CLASSES, URLS) / (url_deg + 1.0)
        url_rounded = url_labels.astype(jnp.bfloat16).reshape(CLASSES, url_blocks, TILE)

        def query_step(carry, item):
            block, qrow, ucol, weight = item
            piece = url_rounded[:, ucol, :]
            term = jnp.dot(piece, block.T, preferred_element_type=jnp.float32)
            return carry.at[:, qrow, :].add(weight * term), None

        query_sums, _ = lax.scan(query_step, jnp.zeros((CLASSES, query_blocks, TILE), jnp.float32), items)
        spread = query_sums.reshape(CLASSES, queries) / (query_deg + 1.0)
        labels = (1.0 - blend_rate) * spread + blend_rate * seed_weight * seed_map
    return labels, url_labels
```

```python
import functools

import jax
import jax.numpy as jnp
from jax import lax
from jax.experimental import pallas as pl
from jax.experimental.pallas import tpu as pltpu
from jax.sharding import PartitionSpec as P

BC = 8
ITERS = 2
GROUPS = 2

blend_rate = 0.25
seed_weight = 8.0

MESH = pl.DeviceIdType.MESH


def kernel(
    n_row, n_col,
    coords, count, prior, seed_ids, seed_class, tiles_hbm,
    labels_out, url_out,
    tiles, prods, qsend, qgrid, part, cross, summed, rowbuf, ugrid, dsend, drecv,
    udeg_part, udeg_recv, qdeg_part, qdeg_recv, udeg_inv, qdeg_inv, seeds,
    tile_sem, a_send, a_recv, b_send, b_recv, c_send, c_recv, d_send, d_recv, g_send, g_recv,
):
    slots, side = tiles.shape[0], tiles.shape[1]
    groups, members = qsend.shape[1], qsend.shape[2]
    q_local, u_local = qsend.shape[3], url_out.shape[1]
    q_blocks = qgrid[0][0].shape[0]
    chips = n_row // 2
    q_split, u_split = side // q_local, side // u_local
    row, col = lax.axis_index("row"), lax.axis_index("col")
    chip, core = row // 2, row % 2
    partner = chip * 2 + 1 - core

    def place(ref, index, split, local):
        if split == 1:
            return ref.at[index]
        start = pl.multiple_of((index % split) * local, local)
        return ref.at[index // split, :, pl.ds(start, local)]

    def copy(src, dst, send, recv, **device):
        return pltpu.make_async_remote_copy(
            src_ref=src, dst_ref=dst, send_sem=send, recv_sem=recv,
            device_id=device, device_id_type=MESH,
        )

    started = []

    def go(op):
        op.start()
        started.append(op)

    loads = [
        pltpu.make_async_copy(tiles_hbm.at[k], tiles.at[k], tile_sem.at[k]) for k in range(slots)
    ]
    for load in loads:
        load.start()

    barrier = pltpu.get_barrier_semaphore()
    for step in range(1, n_row):
        pl.semaphore_signal(
            barrier, inc=1, device_id={"row": lax.rem(row + step, n_row)}, device_id_type=MESH
        )
    for step in range(1, n_col):
        pl.semaphore_signal(
            barrier, inc=1, device_id={"col": lax.rem(col + step, n_col)}, device_id_type=MESH
        )

    def send_queries(it, g, values):
        rounded = values.astype(jnp.bfloat16)
        qsend[it, g] = rounded
        here = place(qgrid[it][g], col, q_split, q_local)
        here[...] = rounded

    def start_queries(it, g):
        for step in range(1, n_col):
            go(copy(
                qsend.at[it, g], place(qgrid[it][g], col, q_split, q_local),
                a_send.at[it, g, step], a_recv.at[it, g, step],
                col=lax.rem(col + step, n_col),
            ))

    for g in range(groups):
        send_queries(0, g, prior[g * members:(g + 1) * members, :])
    pl.semaphore_wait(barrier, n_row + n_col - 2)
    for g in range(groups):
        start_queries(0, g)

    weight = [
        [
            jnp.where((coords[k, 1] == b) & (k < count[0]), 1.0, 0.0).astype(jnp.float32)
            for k in range(slots)
        ]
        for b in range(BC)
    ]
    back_weight = [
        [
            jnp.where((coords[k, 0] == a) & (k < count[0]), 1.0, 0.0).astype(jnp.float32)
            for k in range(slots)
        ]
        for a in range(q_blocks)
    ]

    def combine(weights, values):
        total = weights[0] * values(0)
        for k in range(1, slots):
            total = total + weights[k] * values(k)
        return total

    across = (((1,), (1,)), ((), ()))

    ones = jnp.ones((16, side), jnp.bfloat16)
    for k in range(slots):
        loads[k].wait()
        down = jnp.dot(ones, tiles[k], preferred_element_type=jnp.float32)
        along = lax.dot_general(ones, tiles[k], across, preferred_element_type=jnp.float32)
        prods[k, 0:8, :] = down[0:8]
        prods[k, 8:16, :] = along[0:8]
    for b in range(BC):
        total = combine(weight[b], lambda k: prods[k, 0:8, :])
        for i in range(u_split):
            udeg_part[b * u_split + i] = total[:, i * u_local:(i + 1) * u_local]
    for a in range(q_blocks):
        total = combine(back_weight[a], lambda k: prods[k, 8:16, :])
        for i in range(q_split):
            qdeg_part[a * q_split + i] = total[:, i * q_local:(i + 1) * q_local]
    for step in range(1, n_row):
        peer = lax.rem(row + step, n_row)
        go(copy(udeg_part.at[peer], udeg_recv.at[step], g_send.at[0, step], g_recv.at[0, step], row=peer))
    for step in range(1, n_col):
        peer = lax.rem(col + step, n_col)
        go(copy(qdeg_part.at[peer], qdeg_recv.at[step], g_send.at[1, step], g_recv.at[1, step], col=peer))

    seed_count = seed_ids.shape[1]
    offset = (row * n_col + col) * q_local
    classes = groups * members
    class_hit = (
        lax.broadcasted_iota(jnp.int32, (classes, seed_count), 0) == seed_class[...]
    ).astype(jnp.float32).astype(jnp.bfloat16)
    place_hit = (
        lax.broadcasted_iota(jnp.int32, (q_local, seed_count), 0) == seed_ids[...] - offset
    ).astype(jnp.float32).astype(jnp.bfloat16)
    seeds[...] = (blend_rate * seed_weight) * lax.dot_general(
        class_hit, place_hit, across, preferred_element_type=jnp.float32
    )

    for it in range(ITERS):
        for g in range(groups):
            for step in range(1, n_col):
                copy(
                    qsend.at[it, g], place(qgrid[it][g], col, q_split, q_local),
                    a_send.at[it, g, step], a_recv.at[it, g, step], col=col,
                ).wait_recv()
            for k in range(slots):
                prods[k, 0:members, :] = jnp.dot(
                    qgrid[it][g][coords[k, 0]], tiles[k], preferred_element_type=jnp.float32
                )
            for b in range(BC):
                total = combine(weight[b], lambda k: prods[k, 0:members, :])
                for i in range(u_split):
                    owner = b * u_split + i
                    part[it, g, owner % 2, owner // 2] = total[:, i * u_local:(i + 1) * u_local]
            go(copy(
                part.at[it, g, 1 - core], cross.at[it, g], b_send.at[it, g, 0], b_recv.at[it, g, 0],
                row=partner,
            ))
        for g in range(groups):
            copy(
                part.at[it, g, 1 - core], cross.at[it, g], b_send.at[it, g, 0], b_recv.at[it, g, 0],
                row=partner,
            ).wait_recv()
            for step in list(range(1, chips)) + [0]:
                peer = lax.rem(chip + step, chips)
                summed[it, g, step] = part[it, g, core, peer] + cross[it, g, peer]
                if step:
                    go(copy(
                        summed.at[it, g, step], rowbuf.at[it, g, step],
                        b_send.at[it, g, step], b_recv.at[it, g, step], row=peer * 2 + core,
                    ))
        if it == 0:
            total = udeg_part[row]
            for step in range(1, n_row):
                copy(
                    udeg_part.at[step], udeg_recv.at[step], g_send.at[0, step], g_recv.at[0, step],
                    row=row,
                ).wait_recv()
                total = total + udeg_recv[step]
            udeg_inv[...] = 1.0 / (total + 1.0)
        for g in range(groups):
            total = summed[it, g, 0]
            for step in range(1, chips):
                copy(
                    summed.at[it, g, step], rowbuf.at[it, g, step],
                    b_send.at[it, g, step], b_recv.at[it, g, step], row=row,
                ).wait_recv()
                total = total + rowbuf[it, g, step]
            url_labels = total * udeg_inv[0:1, :]
            if it == ITERS - 1:
                url_out[g * members:(g + 1) * members, :] = url_labels
            mine = place(ugrid[it][g], row, u_split, u_local)
            mine[...] = url_labels.astype(jnp.bfloat16)
            for step in range(1, chips):
                peer = lax.rem(chip + step, chips)
                go(copy(mine, mine, c_send.at[it, g, step], c_recv.at[it, g, step], row=peer * 2 + core))
            go(copy(mine, mine, c_send.at[it, g, 0], c_recv.at[it, g, 0], row=partner))
        for g in range(groups):
            for step in range(1, chips):
                source = lax.rem(chip + chips - step, chips) * 2 + core
                piece = place(ugrid[it][g], source, u_split, u_local)
                copy(piece, piece, c_send.at[it, g, step], c_recv.at[it, g, step], row=row).wait_recv()
                go(copy(
                    piece, piece, c_send.at[it, g, chips + step], c_recv.at[it, g, chips + step],
                    row=partner,
                ))
        if it == 0:
            total = qdeg_part[col]
            for step in range(1, n_col):
                copy(
                    qdeg_part.at[step], qdeg_recv.at[step], g_send.at[1, step], g_recv.at[1, step],
                    col=col,
                ).wait_recv()
                total = total + qdeg_recv[step]
            qdeg_inv[...] = (1.0 - blend_rate) / (total + 1.0)
        for g in range(groups):
            for step in range(chips):
                source = lax.rem(chip + chips - step, chips) * 2 + 1 - core
                piece = place(ugrid[it][g], source, u_split, u_local)
                index = chips + step if step else 0
                copy(piece, piece, c_send.at[it, g, index], c_recv.at[it, g, index], row=row).wait_recv()
            for k in range(slots):
                prods[k, 0:members, :] = lax.dot_general(
                    ugrid[it][g][coords[k, 1]], tiles[k], across,
                    preferred_element_type=jnp.float32,
                )
            for a in range(q_blocks):
                total = combine(back_weight[a], lambda k: prods[k, 0:members, :])
                for i in range(q_split):
                    dsend[it, g, a * q_split + i] = total[:, i * q_local:(i + 1) * q_local]
            for step in range(1, n_col):
                peer = lax.rem(col + step, n_col)
                go(copy(
                    dsend.at[it, g, peer], drecv.at[it, g, step],
                    d_send.at[it, g, step], d_recv.at[it, g, step], col=peer,
                ))
        for g in range(groups):
            total = dsend[it, g, col]
            for step in range(1, n_col):
                copy(
                    dsend.at[it, g, step], drecv.at[it, g, step],
                    d_send.at[it, g, step], d_recv.at[it, g, step], col=col,
                ).wait_recv()
                total = total + drecv[it, g, step]
            rows = slice(g * members, (g + 1) * members)
            labels = total * qdeg_inv[0:1, :] + seeds[rows, :]
            if it == ITERS - 1:
                labels_out[rows, :] = labels
            else:
                send_queries(it + 1, g, labels)
                start_queries(it + 1, g)
    for op in started:
        op.wait_send()


def shards(click_tiles, tile_coords, tile_count, prior_labels, seed_ids, seed_class):
    n_row, n_col = lax.axis_size("row"), lax.axis_size("col")
    slots, side = click_tiles.shape[0], click_tiles.shape[1]
    classes, q_local = prior_labels.shape
    q_blocks = q_local * n_col // side
    u_local = BC * side // n_row
    groups = GROUPS
    members = classes // groups
    chips = n_row // 2
    lead = (ITERS, groups)
    f32, bf16 = jnp.float32, jnp.bfloat16
    vmem = pl.BlockSpec(memory_space=pltpu.VMEM)
    smem = pl.BlockSpec(memory_space=pltpu.SMEM)
    scratch = [
        pltpu.VMEM((slots, side, side), bf16),
        pltpu.VMEM((slots, max(members, 16), side), f32),
        pltpu.VMEM(lead + (members, q_local), bf16),
        [[pltpu.VMEM((q_blocks, members, side), bf16)] * groups] * ITERS,
        pltpu.VMEM(lead + (2, chips, members, u_local), f32),
        pltpu.VMEM(lead + (chips, members, u_local), f32),
        pltpu.VMEM(lead + (chips, members, u_local), f32),
        pltpu.VMEM(lead + (chips, members, u_local), f32),
        [[pltpu.VMEM((BC, members, side), bf16)] * groups] * ITERS,
        pltpu.VMEM(lead + (n_col, members, q_local), f32),
        pltpu.VMEM(lead + (n_col, members, q_local), f32),
        pltpu.VMEM((n_row, 8, u_local), f32),
        pltpu.VMEM((n_row, 8, u_local), f32),
        pltpu.VMEM((n_col, 8, q_local), f32),
        pltpu.VMEM((n_col, 8, q_local), f32),
        pltpu.VMEM((8, u_local), f32),
        pltpu.VMEM((8, q_local), f32),
        pltpu.VMEM((classes, q_local), f32),
        pltpu.SemaphoreType.DMA((slots,)),
        pltpu.SemaphoreType.DMA(lead + (n_col,)),
        pltpu.SemaphoreType.DMA(lead + (n_col,)),
        pltpu.SemaphoreType.DMA(lead + (chips,)),
        pltpu.SemaphoreType.DMA(lead + (chips,)),
        pltpu.SemaphoreType.DMA(lead + (2 * chips,)),
        pltpu.SemaphoreType.DMA(lead + (2 * chips,)),
        pltpu.SemaphoreType.DMA(lead + (n_col,)),
        pltpu.SemaphoreType.DMA(lead + (n_col,)),
        pltpu.SemaphoreType.DMA((2, max(n_row, n_col))),
        pltpu.SemaphoreType.DMA((2, max(n_row, n_col))),
    ]
    return pl.pallas_call(
        functools.partial(kernel, n_row, n_col),
        out_shape=(
            jax.ShapeDtypeStruct((classes, q_local), f32),
            jax.ShapeDtypeStruct((classes, u_local), f32),
        ),
        in_specs=[smem, smem, vmem, vmem, vmem, pl.BlockSpec(memory_space=pl.ANY)],
        out_specs=(vmem, vmem),
        scratch_shapes=scratch,
        compiler_params=pltpu.CompilerParams(
            collective_id=0, has_side_effects=True, vmem_limit_bytes=48 * 1024 * 1024
        ),
    )(tile_coords, tile_count, prior_labels, seed_ids[None, :], seed_class[None, :], click_tiles)


def solution(mesh):
    placed = (
        P(("row", "col"), None, None),
        P(("row", "col"), None),
        P(("row", "col")),
        P(None, ("row", "col")),
        P(("row", "col")),
        P(("row", "col")),
    )
    return jax.shard_map(
        shards,
        mesh=mesh,
        in_specs=placed,
        out_specs=(P(None, ("row", "col")), P(None, ("col", "row"))),
        check_vma=False,
    )
```

```python
import functools

import jax
import jax.numpy as jnp
from jax import lax
from jax.experimental import pallas as pl
from jax.experimental.pallas import tpu as pltpu
from jax.sharding import PartitionSpec as P

BC = 8
ITERS = 2
GROUPS = 4
SKEW = 1

blend_rate = 0.25
seed_weight = 8.0

MESH = pl.DeviceIdType.MESH


def kernel(
    n_row, n_col,
    coords_hbm, count_hbm, prior_hbm, seed_ids_hbm, seed_class_hbm, tiles_hbm,
    labels_out, url_out,
    tiles, prods, qsend, qgrid, part, cross, summed, rowbuf, ugrid, dsend, drecv,
    udeg_part, udeg_recv, qdeg_part, qdeg_recv, udeg_inv, qdeg_inv, seeds,
    coords, count, prior, seed_ids, seed_class, small_sem,
    tile_sem, a_send, a_recv, b_send, b_recv, c_send, c_recv, d_send, d_recv, g_send, g_recv,
):
    slots, side = tiles.shape[0], tiles.shape[1]
    groups, members = qsend.shape[1], qsend.shape[2]
    q_local, u_local = qsend.shape[3], url_out.shape[1]
    q_blocks = qgrid[0][0].shape[0]
    chips = n_row // 2
    q_split, u_split = side // q_local, side // u_local
    row, col = lax.axis_index("row"), lax.axis_index("col")
    chip, core = row // 2, row % 2
    partner = chip * 2 + 1 - core

    def place(ref, index, split, local):
        if split == 1:
            return ref.at[index]
        start = pl.multiple_of((index % split) * local, local)
        return ref.at[index // split, :, pl.ds(start, local)]

    def copy(src, dst, send, recv, **device):
        return pltpu.make_async_remote_copy(
            src_ref=src, dst_ref=dst, send_sem=send, recv_sem=recv,
            device_id=device, device_id_type=MESH,
        )

    started = []

    def go(op):
        op.start()
        started.append(op)

    small = [
        pltpu.make_async_copy(source, target, small_sem.at[i])
        for i, (source, target) in enumerate((
            (prior_hbm, prior), (coords_hbm, coords), (count_hbm, count),
            (seed_ids_hbm, seed_ids), (seed_class_hbm, seed_class),
        ))
    ]
    for load in small:
        load.start()
    loads = [
        pltpu.make_async_copy(tiles_hbm.at[k], tiles.at[k], tile_sem.at[k]) for k in range(slots)
    ]
    for load in loads:
        load.start()

    barrier = pltpu.get_barrier_semaphore()
    for step in range(1, n_row):
        pl.semaphore_signal(
            barrier, inc=1, device_id={"row": lax.rem(row + step, n_row)}, device_id_type=MESH
        )
    for step in range(1, n_col):
        pl.semaphore_signal(
            barrier, inc=1, device_id={"col": lax.rem(col + step, n_col)}, device_id_type=MESH
        )

    def send_queries(it, g, values):
        rounded = values.astype(jnp.bfloat16)
        qsend[it, g] = rounded
        here = place(qgrid[it][g], col, q_split, q_local)
        here[...] = rounded

    def start_queries(it, g):
        for step in range(1, n_col):
            go(copy(
                qsend.at[it, g], place(qgrid[it][g], col, q_split, q_local),
                a_send.at[it, g, step], a_recv.at[it, g, step],
                col=lax.rem(col + step, n_col),
            ))

    for load in small:
        load.wait()
    for g in range(groups):
        send_queries(0, g, prior[g * members:(g + 1) * members, :])
    pl.semaphore_wait(barrier, n_row + n_col - 2)
    for g in range(groups):
        start_queries(0, g)

    weight = [
        [
            jnp.where((coords[1, k] == b) & (k < count[0, 0]), 1.0, 0.0).astype(jnp.float32)
            for k in range(slots)
        ]
        for b in range(BC)
    ]
    back_weight = [
        [
            jnp.where((coords[0, k] == a) & (k < count[0, 0]), 1.0, 0.0).astype(jnp.float32)
            for k in range(slots)
        ]
        for a in range(q_blocks)
    ]

    def combine(weights, values):
        total = weights[0] * values(0)
        for k in range(1, slots):
            total = total + weights[k] * values(k)
        return total

    across = (((1,), (1,)), ((), ()))

    ones = jnp.ones((16, side), jnp.bfloat16)
    for k in range(slots):
        loads[k].wait()
        down = jnp.dot(ones, tiles[k], preferred_element_type=jnp.float32)
        along = lax.dot_general(ones, tiles[k], across, preferred_element_type=jnp.float32)
        prods[k, 0:8, :] = down[0:8]
        prods[k, 8:16, :] = along[0:8]
    for b in range(BC):
        total = combine(weight[b], lambda k: prods[k, 0:8, :])
        for i in range(u_split):
            udeg_part[b * u_split + i] = total[:, i * u_local:(i + 1) * u_local]
    qdeg_part[...] = jnp.zeros_like(qdeg_part)
    for a in range(q_blocks):
        total = combine(back_weight[a], lambda k: prods[k, 8:16, :])
        for i in range(q_split):
            qdeg_part[pl.ds(a * q_split + i, 1), :] = total[0:1, i * q_local:(i + 1) * q_local]
    for step in range(1, n_row):
        peer = lax.rem(row + step, n_row)
        go(copy(udeg_part.at[peer], udeg_recv.at[step], g_send.at[0, step], g_recv.at[0, step], row=peer))
    for step in range(1, n_col):
        peer = lax.rem(col + step, n_col)
        go(copy(qdeg_part, qdeg_recv.at[step], g_send.at[1, step], g_recv.at[1, step], col=peer))

    seed_count = seed_ids.shape[1]
    offset = (row * n_col + col) * q_local
    classes = groups * members
    class_hit = (
        lax.broadcasted_iota(jnp.int32, (classes, seed_count), 0) == seed_class[...]
    ).astype(jnp.float32).astype(jnp.bfloat16)
    place_hit = (
        lax.broadcasted_iota(jnp.int32, (q_local, seed_count), 0) == seed_ids[...] - offset
    ).astype(jnp.float32).astype(jnp.bfloat16)
    seeds[...] = (blend_rate * seed_weight) * lax.dot_general(
        class_hit, place_hit, across, preferred_element_type=jnp.float32
    )

    def finish_url_degrees():
        total = udeg_part[row]
        for step in range(1, n_row):
            copy(
                udeg_part.at[step], udeg_recv.at[step], g_send.at[0, step], g_recv.at[0, step],
                row=row,
            ).wait_recv()
            total = total + udeg_recv[step]
        udeg_inv[...] = 1.0 / (total + 1.0)

    def finish_query_degrees():
        total = qdeg_part[...]
        for step in range(1, n_col):
            copy(
                qdeg_part, qdeg_recv.at[step], g_send.at[1, step], g_recv.at[1, step],
                col=col,
            ).wait_recv()
            total = total + qdeg_recv[step]
        qdeg_inv[...] = (1.0 - blend_rate) / (total + 1.0)

    def flow(g):
        for it in range(ITERS):
            yield
            for step in range(1, n_col):
                copy(
                    qsend.at[it, g], place(qgrid[it][g], col, q_split, q_local),
                    a_send.at[it, g, step], a_recv.at[it, g, step], col=col,
                ).wait_recv()
            for k in range(slots):
                prods[k, 0:members, :] = jnp.dot(
                    qgrid[it][g][coords[0, k]], tiles[k], preferred_element_type=jnp.float32
                )
            for b in range(BC):
                total = combine(weight[b], lambda k: prods[k, 0:members, :])
                for i in range(u_split):
                    owner = b * u_split + i
                    part[it, g, owner % 2, owner // 2] = total[:, i * u_local:(i + 1) * u_local]
            go(copy(
                part.at[it, g, 1 - core], cross.at[it, g], b_send.at[it, g, 0], b_recv.at[it, g, 0],
                row=partner,
            ))
            yield
            copy(
                part.at[it, g, 1 - core], cross.at[it, g], b_send.at[it, g, 0], b_recv.at[it, g, 0],
                row=partner,
            ).wait_recv()
            for step in list(range(1, chips)) + [0]:
                peer = lax.rem(chip + step, chips)
                summed[it, g, step] = part[it, g, core, peer] + cross[it, g, peer]
                if step:
                    go(copy(
                        summed.at[it, g, step], rowbuf.at[it, g, step],
                        b_send.at[it, g, step], b_recv.at[it, g, step], row=peer * 2 + core,
                    ))
            if it == 0 and g == 0:
                finish_url_degrees()
            yield
            total = summed[it, g, 0]
            for step in range(1, chips):
                copy(
                    summed.at[it, g, step], rowbuf.at[it, g, step],
                    b_send.at[it, g, step], b_recv.at[it, g, step], row=row,
                ).wait_recv()
                total = total + rowbuf[it, g, step]
            url_labels = total * udeg_inv[0:1, :]
            if it == ITERS - 1:
                url_out[g * members:(g + 1) * members, :] = url_labels
            mine = place(ugrid[it][g], row, u_split, u_local)
            mine[...] = url_labels.astype(jnp.bfloat16)
            for step in range(1, chips):
                peer = lax.rem(chip + step, chips)
                go(copy(mine, mine, c_send.at[it, g, step], c_recv.at[it, g, step], row=peer * 2 + core))
            go(copy(mine, mine, c_send.at[it, g, 0], c_recv.at[it, g, 0], row=partner))
            yield
            for step in range(1, chips):
                source = lax.rem(chip + chips - step, chips) * 2 + core
                piece = place(ugrid[it][g], source, u_split, u_local)
                copy(piece, piece, c_send.at[it, g, step], c_recv.at[it, g, step], row=row).wait_recv()
                go(copy(
                    piece, piece, c_send.at[it, g, chips + step], c_recv.at[it, g, chips + step],
                    row=partner,
                ))
            if it == 0 and g == 0:
                finish_query_degrees()
            yield
            for step in range(chips):
                source = lax.rem(chip + chips - step, chips) * 2 + 1 - core
                piece = place(ugrid[it][g], source, u_split, u_local)
                index = chips + step if step else 0
                copy(piece, piece, c_send.at[it, g, index], c_recv.at[it, g, index], row=row).wait_recv()
            for k in range(slots):
                prods[k, 0:members, :] = lax.dot_general(
                    ugrid[it][g][coords[1, k]], tiles[k], across,
                    preferred_element_type=jnp.float32,
                )
            for a in range(q_blocks):
                total = combine(back_weight[a], lambda k: prods[k, 0:members, :])
                for i in range(q_split):
                    owner = a * q_split + i
                    scaled = total[:, i * q_local:(i + 1) * q_local] * qdeg_inv[owner:owner + 1, :]
                    dsend[it, g, owner] = scaled
            for step in range(1, n_col):
                peer = lax.rem(col + step, n_col)
                go(copy(
                    dsend.at[it, g, peer], drecv.at[it, g, step],
                    d_send.at[it, g, step], d_recv.at[it, g, step], col=peer,
                ))
            yield
            total = dsend[it, g, col]
            for step in range(1, n_col):
                copy(
                    dsend.at[it, g, step], drecv.at[it, g, step],
                    d_send.at[it, g, step], d_recv.at[it, g, step], col=col,
                ).wait_recv()
                total = total + drecv[it, g, step]
            rows = slice(g * members, (g + 1) * members)
            labels = total + seeds[rows, :]
            if it == ITERS - 1:
                labels_out[rows, :] = labels
            else:
                send_queries(it + 1, g, labels)
                start_queries(it + 1, g)
        yield

    stages = 6 * ITERS
    flows = [flow(g) for g in range(groups)]
    for g in range(groups):
        next(flows[g])
    for slot in range(stages + SKEW * (groups - 1)):
        for g in range(groups):
            if 0 <= slot - SKEW * g < stages:
                next(flows[g])
    for op in started:
        op.wait_send()


def shards(click_tiles, tile_coords, tile_count, prior_labels, seed_ids, seed_class):
    n_row, n_col = lax.axis_size("row"), lax.axis_size("col")
    slots, side = click_tiles.shape[0], click_tiles.shape[1]
    classes, q_local = prior_labels.shape
    q_blocks = q_local * n_col // side
    u_local = BC * side // n_row
    groups = GROUPS
    members = classes // groups
    chips = n_row // 2
    lead = (ITERS, groups)
    f32, bf16 = jnp.float32, jnp.bfloat16
    vmem = pl.BlockSpec(memory_space=pltpu.VMEM)
    scratch = [
        pltpu.VMEM((slots, side, side), bf16),
        pltpu.VMEM((slots, max(members, 16), side), f32),
        pltpu.VMEM(lead + (members, q_local), bf16),
        [[pltpu.VMEM((q_blocks, members, side), bf16)] * groups] * ITERS,
        pltpu.VMEM(lead + (2, chips, members, u_local), f32),
        pltpu.VMEM(lead + (chips, members, u_local), f32),
        pltpu.VMEM(lead + (chips, members, u_local), f32),
        pltpu.VMEM(lead + (chips, members, u_local), f32),
        [[pltpu.VMEM((BC, members, side), bf16)] * groups] * ITERS,
        pltpu.VMEM(lead + (n_col, members, q_local), f32),
        pltpu.VMEM(lead + (n_col, members, q_local), f32),
        pltpu.VMEM((n_row, 8, u_local), f32),
        pltpu.VMEM((n_row, 8, u_local), f32),
        pltpu.VMEM((max(n_col, 8), q_local), f32),
        pltpu.VMEM((n_col, max(n_col, 8), q_local), f32),
        pltpu.VMEM((8, u_local), f32),
        pltpu.VMEM((max(n_col, 8), q_local), f32),
        pltpu.VMEM((classes, q_local), f32),
        pltpu.SMEM((2, slots), jnp.int32),
        pltpu.SMEM((1, 1), jnp.int32),
        pltpu.VMEM((classes, q_local), f32),
        pltpu.VMEM((1, seed_ids.shape[0]), jnp.int32),
        pltpu.VMEM((1, seed_ids.shape[0]), jnp.int32),
        pltpu.SemaphoreType.DMA((5,)),
        pltpu.SemaphoreType.DMA((slots,)),
        pltpu.SemaphoreType.DMA(lead + (n_col,)),
        pltpu.SemaphoreType.DMA(lead + (n_col,)),
        pltpu.SemaphoreType.DMA(lead + (chips,)),
        pltpu.SemaphoreType.DMA(lead + (chips,)),
        pltpu.SemaphoreType.DMA(lead + (2 * chips,)),
        pltpu.SemaphoreType.DMA(lead + (2 * chips,)),
        pltpu.SemaphoreType.DMA(lead + (n_col,)),
        pltpu.SemaphoreType.DMA(lead + (n_col,)),
        pltpu.SemaphoreType.DMA((2, max(n_row, n_col))),
        pltpu.SemaphoreType.DMA((2, max(n_row, n_col))),
    ]
    return pl.pallas_call(
        functools.partial(kernel, n_row, n_col),
        out_shape=(
            jax.ShapeDtypeStruct((classes, q_local), f32),
            jax.ShapeDtypeStruct((classes, u_local), f32),
        ),
        in_specs=[pl.BlockSpec(memory_space=pl.ANY)] * 6,
        out_specs=(vmem, vmem),
        scratch_shapes=scratch,
        compiler_params=pltpu.CompilerParams(
            collective_id=0, has_side_effects=True, vmem_limit_bytes=60 * 1024 * 1024
        ),
    )(tile_coords.T, tile_count[None, :], prior_labels, seed_ids[None, :], seed_class[None, :], click_tiles)


def solution(mesh):
    placed = (
        P(("row", "col"), None, None),
        P(("row", "col"), None),
        P(("row", "col")),
        P(None, ("row", "col")),
        P(("row", "col")),
        P(("row", "col")),
    )
    return jax.shard_map(
        shards,
        mesh=mesh,
        in_specs=placed,
        out_specs=(P(None, ("row", "col")), P(None, ("col", "row"))),
        check_vma=False,
    )
```

```python
import functools

import jax
import jax.numpy as jnp
from jax import lax
from jax.experimental import pallas as pl
from jax.experimental.pallas import tpu as pltpu
from jax.sharding import PartitionSpec as P

BC = 8
ITERS = 2
GROUPS = 2

blend_rate = 0.25
seed_weight = 8.0

MESH = pl.DeviceIdType.MESH


def kernel(
    n_row, n_col,
    coords_hbm, count_hbm, prior_hbm, seed_ids_hbm, seed_class_hbm, tiles_hbm,
    labels_out, url_out,
    tiles, prods, qsend, qgrid, part, cross, summed, rowbuf, ugrid, dsend, drecv,
    udeg_part, udeg_recv, qdeg_part, qdeg_recv, udeg_inv, qdeg_inv, seeds,
    coords, count, prior, seed_ids, seed_class, small_sem,
    tile_sem, a_send, a_recv, b_send, b_recv, c_send, c_recv, d_send, d_recv, g_send, g_recv,
):
    slots, side = tiles.shape[0], tiles.shape[1]
    groups, members = qsend.shape[1], qsend.shape[2]
    q_local, u_local = qsend.shape[3], url_out.shape[1]
    q_blocks = qgrid[0][0].shape[0]
    chips = n_row // 2
    q_split, u_split = side // q_local, side // u_local
    row, col = lax.axis_index("row"), lax.axis_index("col")
    chip, core = row // 2, row % 2
    partner = chip * 2 + 1 - core

    def place(ref, index, split, local):
        if split == 1:
            return ref.at[index]
        start = pl.multiple_of((index % split) * local, local)
        return ref.at[index // split, :, pl.ds(start, local)]

    def copy(src, dst, send, recv, **device):
        return pltpu.make_async_remote_copy(
            src_ref=src, dst_ref=dst, send_sem=send, recv_sem=recv,
            device_id=device, device_id_type=MESH,
        )

    started = []

    def go(op):
        op.start()
        started.append(op)

    small = [
        pltpu.make_async_copy(source, target, small_sem.at[i])
        for i, (source, target) in enumerate((
            (prior_hbm, prior), (coords_hbm, coords), (count_hbm, count),
            (seed_ids_hbm, seed_ids), (seed_class_hbm, seed_class),
        ))
    ]
    for load in small:
        load.start()
    loads = [
        pltpu.make_async_copy(tiles_hbm.at[k], tiles.at[k], tile_sem.at[k]) for k in range(slots)
    ]
    for load in loads:
        load.start()

    barrier = pltpu.get_barrier_semaphore()
    for step in range(1, n_row):
        pl.semaphore_signal(
            barrier, inc=1, device_id={"row": lax.rem(row + step, n_row)}, device_id_type=MESH
        )
    for step in range(1, n_col):
        pl.semaphore_signal(
            barrier, inc=1, device_id={"col": lax.rem(col + step, n_col)}, device_id_type=MESH
        )

    def send_queries(it, g, values):
        rounded = values.astype(jnp.bfloat16)
        qsend[it, g] = rounded
        here = place(qgrid[it][g], col, q_split, q_local)
        here[...] = rounded

    def start_queries(it, g):
        for step in range(1, n_col):
            go(copy(
                qsend.at[it, g], place(qgrid[it][g], col, q_split, q_local),
                a_send.at[it, g, step], a_recv.at[it, g, step],
                col=lax.rem(col + step, n_col),
            ))

    for load in small:
        load.wait()
    for g in range(groups):
        send_queries(0, g, prior[g * members:(g + 1) * members, :])
    pl.semaphore_wait(barrier, n_row + n_col - 2)
    for g in range(groups):
        start_queries(0, g)

    weight = [
        [
            jnp.where((coords[1, k] == b) & (k < count[0, 0]), 1.0, 0.0).astype(jnp.float32)
            for k in range(slots)
        ]
        for b in range(BC)
    ]
    back_weight = [
        [
            jnp.where((coords[0, k] == a) & (k < count[0, 0]), 1.0, 0.0).astype(jnp.float32)
            for k in range(slots)
        ]
        for a in range(q_blocks)
    ]

    def combine(weights, values):
        total = weights[0] * values(0)
        for k in range(1, slots):
            total = total + weights[k] * values(k)
        return total

    across = (((1,), (1,)), ((), ()))
    ones = jnp.ones((16, side), jnp.bfloat16)

    def lead_rows(it, g, value):
        return jnp.concatenate([value, ones], axis=0) if it == 0 and g == 0 else value

    seed_count = seed_ids.shape[1]
    offset = (row * n_col + col) * q_local
    classes = groups * members
    class_hit = (
        lax.broadcasted_iota(jnp.int32, (classes, seed_count), 0) == seed_class[...]
    ).astype(jnp.float32).astype(jnp.bfloat16)
    place_hit = (
        lax.broadcasted_iota(jnp.int32, (q_local, seed_count), 0) == seed_ids[...] - offset
    ).astype(jnp.float32).astype(jnp.bfloat16)
    seeds[...] = (blend_rate * seed_weight) * lax.dot_general(
        class_hit, place_hit, across, preferred_element_type=jnp.float32
    )

    def finish_url_degrees():
        total = udeg_part[row]
        for step in range(1, n_row):
            copy(
                udeg_part.at[step], udeg_recv.at[step], g_send.at[0, step], g_recv.at[0, step],
                row=row,
            ).wait_recv()
            total = total + udeg_recv[step]
        udeg_inv[...] = 1.0 / (total + 1.0)

    def finish_query_degrees():
        total = qdeg_part[col]
        for step in range(1, n_col):
            copy(
                qdeg_part.at[step], qdeg_recv.at[step], g_send.at[1, step], g_recv.at[1, step],
                col=col,
            ).wait_recv()
            total = total + qdeg_recv[step]
        qdeg_inv[...] = (1.0 - blend_rate) / (total + 1.0)

    def flow(g):
        for it in range(ITERS):
            yield
            for step in range(1, n_col):
                copy(
                    qsend.at[it, g], place(qgrid[it][g], col, q_split, q_local),
                    a_send.at[it, g, step], a_recv.at[it, g, step], col=col,
                ).wait_recv()
            for k in range(slots):
                if it == 0 and g == 0:
                    loads[k].wait()
                product = jnp.dot(
                    lead_rows(it, g, qgrid[it][g][coords[0, k]]), tiles[k],
                    preferred_element_type=jnp.float32,
                )
                prods[k, 0:product.shape[0], :] = product
            for b in range(BC):
                total = combine(weight[b], lambda k: prods[k, 0:members, :])
                for i in range(u_split):
                    owner = b * u_split + i
                    part[it, g, owner % 2, owner // 2] = total[:, i * u_local:(i + 1) * u_local]
            go(copy(
                part.at[it, g, 1 - core], cross.at[it, g], b_send.at[it, g, 0], b_recv.at[it, g, 0],
                row=partner,
            ))
            if it == 0 and g == 0:
                for b in range(BC):
                    total = combine(weight[b], lambda k: prods[k, members:members + 8, :])
                    for i in range(u_split):
                        udeg_part[b * u_split + i] = total[:, i * u_local:(i + 1) * u_local]
                for step in range(1, n_row):
                    peer = lax.rem(row + step, n_row)
                    go(copy(
                        udeg_part.at[peer], udeg_recv.at[step],
                        g_send.at[0, step], g_recv.at[0, step], row=peer,
                    ))
            yield
            copy(
                part.at[it, g, 1 - core], cross.at[it, g], b_send.at[it, g, 0], b_recv.at[it, g, 0],
                row=partner,
            ).wait_recv()
            for step in list(range(1, chips)) + [0]:
                peer = lax.rem(chip + step, chips)
                summed[it, g, step] = part[it, g, core, peer] + cross[it, g, peer]
                if step:
                    go(copy(
                        summed.at[it, g, step], rowbuf.at[it, g, step],
                        b_send.at[it, g, step], b_recv.at[it, g, step], row=peer * 2 + core,
                    ))
            yield
            if it == 0 and g == 0:
                finish_url_degrees()
            total = summed[it, g, 0]
            for step in range(1, chips):
                copy(
                    summed.at[it, g, step], rowbuf.at[it, g, step],
                    b_send.at[it, g, step], b_recv.at[it, g, step], row=row,
                ).wait_recv()
                total = total + rowbuf[it, g, step]
            url_labels = total * udeg_inv[0:1, :]
            if it == ITERS - 1:
                url_out[g * members:(g + 1) * members, :] = url_labels
            mine = place(ugrid[it][g], row, u_split, u_local)
            mine[...] = url_labels.astype(jnp.bfloat16)
            for step in range(1, chips):
                peer = lax.rem(chip + step, chips)
                go(copy(mine, mine, c_send.at[it, g, step], c_recv.at[it, g, step], row=peer * 2 + core))
            go(copy(mine, mine, c_send.at[it, g, 0], c_recv.at[it, g, 0], row=partner))
            yield
            for step in range(1, chips):
                source = lax.rem(chip + chips - step, chips) * 2 + core
                piece = place(ugrid[it][g], source, u_split, u_local)
                copy(piece, piece, c_send.at[it, g, step], c_recv.at[it, g, step], row=row).wait_recv()
                go(copy(
                    piece, piece, c_send.at[it, g, chips + step], c_recv.at[it, g, chips + step],
                    row=partner,
                ))
            yield
            for step in range(chips):
                source = lax.rem(chip + chips - step, chips) * 2 + 1 - core
                piece = place(ugrid[it][g], source, u_split, u_local)
                index = chips + step if step else 0
                copy(piece, piece, c_send.at[it, g, index], c_recv.at[it, g, index], row=row).wait_recv()
            for k in range(slots):
                product = lax.dot_general(
                    lead_rows(it, g, ugrid[it][g][coords[1, k]]), tiles[k], across,
                    preferred_element_type=jnp.float32,
                )
                prods[k, 0:product.shape[0], :] = product
            for a in range(q_blocks):
                total = combine(back_weight[a], lambda k: prods[k, 0:members, :])
                for i in range(q_split):
                    owner = a * q_split + i
                    dsend[it, g, owner] = total[:, i * q_local:(i + 1) * q_local]
            for step in range(1, n_col):
                peer = lax.rem(col + step, n_col)
                go(copy(
                    dsend.at[it, g, peer], drecv.at[it, g, step],
                    d_send.at[it, g, step], d_recv.at[it, g, step], col=peer,
                ))
            if it == 0 and g == 0:
                for a in range(q_blocks):
                    total = combine(back_weight[a], lambda k: prods[k, members:members + 8, :])
                    for i in range(q_split):
                        qdeg_part[a * q_split + i] = total[:, i * q_local:(i + 1) * q_local]
                for step in range(1, n_col):
                    peer = lax.rem(col + step, n_col)
                    go(copy(
                        qdeg_part.at[peer], qdeg_recv.at[step],
                        g_send.at[1, step], g_recv.at[1, step], col=peer,
                    ))
            yield
            if it == 0 and g == 0:
                finish_query_degrees()
            total = dsend[it, g, col]
            for step in range(1, n_col):
                copy(
                    dsend.at[it, g, step], drecv.at[it, g, step],
                    d_send.at[it, g, step], d_recv.at[it, g, step], col=col,
                ).wait_recv()
                total = total + drecv[it, g, step]
            rows = slice(g * members, (g + 1) * members)
            labels = total * qdeg_inv[0:1, :] + seeds[rows, :]
            if it == ITERS - 1:
                labels_out[rows, :] = labels
            else:
                send_queries(it + 1, g, labels)
                start_queries(it + 1, g)
        yield

    flows = [flow(g) for g in range(groups)]
    for g in range(groups):
        next(flows[g])
    for it in range(ITERS):
        for stages in ((0,), (1,), (2,), (3, 4), (5,)):
            for g in range(groups):
                for stage in stages:
                    next(flows[g])
    for op in started:
        op.wait_send()


def shards(click_tiles, tile_coords, tile_count, prior_labels, seed_ids, seed_class):
    n_row, n_col = lax.axis_size("row"), lax.axis_size("col")
    slots, side = click_tiles.shape[0], click_tiles.shape[1]
    classes, q_local = prior_labels.shape
    q_blocks = q_local * n_col // side
    u_local = BC * side // n_row
    groups = GROUPS
    members = classes // groups
    chips = n_row // 2
    lead = (ITERS, groups)
    f32, bf16 = jnp.float32, jnp.bfloat16
    vmem = pl.BlockSpec(memory_space=pltpu.VMEM)
    scratch = [
        pltpu.VMEM((slots, side, side), bf16),
        pltpu.VMEM((slots, members + 16, side), f32),
        pltpu.VMEM(lead + (members, q_local), bf16),
        [[pltpu.VMEM((q_blocks, members, side), bf16)] * groups] * ITERS,
        pltpu.VMEM(lead + (2, chips, members, u_local), f32),
        pltpu.VMEM(lead + (chips, members, u_local), f32),
        pltpu.VMEM(lead + (chips, members, u_local), f32),
        pltpu.VMEM(lead + (chips, members, u_local), f32),
        [[pltpu.VMEM((BC, members, side), bf16)] * groups] * ITERS,
        pltpu.VMEM(lead + (n_col, members, q_local), f32),
        pltpu.VMEM(lead + (n_col, members, q_local), f32),
        pltpu.VMEM((n_row, 8, u_local), f32),
        pltpu.VMEM((n_row, 8, u_local), f32),
        pltpu.VMEM((n_col, 8, q_local), f32),
        pltpu.VMEM((n_col, 8, q_local), f32),
        pltpu.VMEM((8, u_local), f32),
        pltpu.VMEM((8, q_local), f32),
        pltpu.VMEM((classes, q_local), f32),
        pltpu.SMEM((2, slots), jnp.int32),
        pltpu.SMEM((1, 1), jnp.int32),
        pltpu.VMEM((classes, q_local), f32),
        pltpu.VMEM((1, seed_ids.shape[0]), jnp.int32),
        pltpu.VMEM((1, seed_ids.shape[0]), jnp.int32),
        pltpu.SemaphoreType.DMA((5,)),
        pltpu.SemaphoreType.DMA((slots,)),
        pltpu.SemaphoreType.DMA(lead + (n_col,)),
        pltpu.SemaphoreType.DMA(lead + (n_col,)),
        pltpu.SemaphoreType.DMA(lead + (chips,)),
        pltpu.SemaphoreType.DMA(lead + (chips,)),
        pltpu.SemaphoreType.DMA(lead + (2 * chips,)),
        pltpu.SemaphoreType.DMA(lead + (2 * chips,)),
        pltpu.SemaphoreType.DMA(lead + (n_col,)),
        pltpu.SemaphoreType.DMA(lead + (n_col,)),
        pltpu.SemaphoreType.DMA((2, max(n_row, n_col))),
        pltpu.SemaphoreType.DMA((2, max(n_row, n_col))),
    ]
    return pl.pallas_call(
        functools.partial(kernel, n_row, n_col),
        out_shape=(
            jax.ShapeDtypeStruct((classes, q_local), f32),
            jax.ShapeDtypeStruct((classes, u_local), f32),
        ),
        in_specs=[pl.BlockSpec(memory_space=pl.ANY)] * 6,
        out_specs=(vmem, vmem),
        scratch_shapes=scratch,
        compiler_params=pltpu.CompilerParams(
            collective_id=0, has_side_effects=True, vmem_limit_bytes=58 * 1024 * 1024
        ),
    )(tile_coords.T, tile_count[None, :], prior_labels, seed_ids[None, :], seed_class[None, :], click_tiles)


def solution(mesh):
    placed = (
        P(("row", "col"), None, None),
        P(("row", "col"), None),
        P(("row", "col")),
        P(None, ("row", "col")),
        P(("row", "col")),
        P(("row", "col")),
    )
    return jax.shard_map(
        shards,
        mesh=mesh,
        in_specs=placed,
        out_specs=(P(None, ("row", "col")), P(None, ("col", "row"))),
        check_vma=False,
    )
```

```python
import functools

import jax
import jax.numpy as jnp
from jax import lax
from jax.experimental import pallas as pl
from jax.experimental.pallas import tpu as pltpu
from jax.sharding import PartitionSpec as P

BC = 8
ITERS = 2
GROUPS = 2
WIRE_TOP = 32767.0
SCALE_LANES = 128
SCALE_STEPS = 256.0

blend_rate = 0.25
seed_weight = 8.0

MESH = pl.DeviceIdType.MESH


def encode(ref, values):
    top = jnp.maximum(jnp.max(values, axis=1, keepdims=True), 1e-30)
    power = jnp.floor(jnp.log2(top) * SCALE_STEPS) + 2.0
    steps = values * (WIRE_TOP * jnp.exp2(power * (-1.0 / SCALE_STEPS))) + 0.5
    width = values.shape[1]
    ref[:, 0:width] = steps.astype(jnp.int32).astype(jnp.int16)
    ref[:, width:width + SCALE_LANES] = jnp.broadcast_to(
        power, (values.shape[0], SCALE_LANES)
    ).astype(jnp.int32).astype(jnp.int16)


def decode(ref, width):
    power = ref[:, width:width + SCALE_LANES].astype(jnp.int32).astype(jnp.float32)
    unit = jnp.exp2(power * (1.0 / SCALE_STEPS)) * (1.0 / WIRE_TOP)
    return ref[:, 0:width].astype(jnp.int32).astype(jnp.float32) * unit[:, 0:1]


def kernel(
    n_row, n_col,
    coords_hbm, count_hbm, prior_hbm, seed_ids_hbm, seed_class_hbm, tiles_hbm,
    labels_out, url_out,
    tiles, prods, qsend, qgrid, part, cross, summed, rowbuf, own, ugrid, dsend, dcode, drecv,
    udeg_part, udeg_recv, qdeg_part, qdeg_recv, udeg_inv, qdeg_inv, seeds,
    coords, count, prior, seed_ids, seed_class, small_sem,
    tile_sem, a_send, a_recv, b_send, b_recv, c_send, c_recv, d_send, d_recv, g_send, g_recv,
):
    slots, side = tiles.shape[0], tiles.shape[1]
    groups, members = qsend.shape[1], qsend.shape[2]
    q_local, u_local = qsend.shape[3], url_out.shape[1]
    q_blocks = qgrid[0][0].shape[0]
    chips = n_row // 2
    q_split, u_split = side // q_local, side // u_local
    row, col = lax.axis_index("row"), lax.axis_index("col")
    chip, core = row // 2, row % 2
    partner = chip * 2 + 1 - core

    def place(ref, index, split, local):
        if split == 1:
            return ref.at[index]
        start = pl.multiple_of((index % split) * local, local)
        return ref.at[index // split, :, pl.ds(start, local)]

    def copy(src, dst, send, recv, **device):
        return pltpu.make_async_remote_copy(
            src_ref=src, dst_ref=dst, send_sem=send, recv_sem=recv,
            device_id=device, device_id_type=MESH,
        )

    started = []

    def go(op):
        op.start()
        started.append(op)

    small = [
        pltpu.make_async_copy(source, target, small_sem.at[i])
        for i, (source, target) in enumerate((
            (prior_hbm, prior), (coords_hbm, coords), (count_hbm, count),
            (seed_ids_hbm, seed_ids), (seed_class_hbm, seed_class),
        ))
    ]
    for load in small:
        load.start()
    loads = [
        pltpu.make_async_copy(tiles_hbm.at[k], tiles.at[k], tile_sem.at[k]) for k in range(slots)
    ]
    for load in loads:
        load.start()

    barrier = pltpu.get_barrier_semaphore()
    for step in range(1, n_row):
        pl.semaphore_signal(
            barrier, inc=1, device_id={"row": lax.rem(row + step, n_row)}, device_id_type=MESH
        )
    for step in range(1, n_col):
        pl.semaphore_signal(
            barrier, inc=1, device_id={"col": lax.rem(col + step, n_col)}, device_id_type=MESH
        )

    def send_queries(it, g, values):
        rounded = values.astype(jnp.bfloat16)
        qsend[it, g] = rounded
        here = place(qgrid[it][g], col, q_split, q_local)
        here[...] = rounded

    def start_queries(it, g):
        for step in range(1, n_col):
            go(copy(
                qsend.at[it, g], place(qgrid[it][g], col, q_split, q_local),
                a_send.at[it, g, step], a_recv.at[it, g, step],
                col=lax.rem(col + step, n_col),
            ))

    for load in small:
        load.wait()
    for g in range(groups):
        send_queries(0, g, prior[g * members:(g + 1) * members, :])
    pl.semaphore_wait(barrier, n_row + n_col - 2)
    for g in range(groups):
        start_queries(0, g)

    weight = [
        [
            jnp.where((coords[1, k] == b) & (k < count[0, 0]), 1.0, 0.0).astype(jnp.float32)
            for k in range(slots)
        ]
        for b in range(BC)
    ]
    back_weight = [
        [
            jnp.where((coords[0, k] == a) & (k < count[0, 0]), 1.0, 0.0).astype(jnp.float32)
            for k in range(slots)
        ]
        for a in range(q_blocks)
    ]

    def combine(weights, values):
        total = weights[0] * values(0)
        for k in range(1, slots):
            total = total + weights[k] * values(k)
        return total

    across = (((1,), (1,)), ((), ()))

    ones = jnp.ones((16, side), jnp.bfloat16)
    for k in range(slots):
        loads[k].wait()
        down = jnp.dot(ones, tiles[k], preferred_element_type=jnp.float32)
        along = lax.dot_general(ones, tiles[k], across, preferred_element_type=jnp.float32)
        prods[k, 0:8, :] = down[0:8]
        prods[k, 8:16, :] = along[0:8]
    for b in range(BC):
        total = combine(weight[b], lambda k: prods[k, 0:8, :])
        for i in range(u_split):
            udeg_part[pl.ds(b * u_split + i, 1), :] = total[0:1, i * u_local:(i + 1) * u_local]
    qdeg_part[...] = jnp.zeros_like(qdeg_part)
    for a in range(q_blocks):
        total = combine(back_weight[a], lambda k: prods[k, 8:16, :])
        for i in range(q_split):
            qdeg_part[pl.ds(a * q_split + i, 1), :] = total[0:1, i * q_local:(i + 1) * q_local]
    for step in range(1, n_row):
        peer = lax.rem(row + step, n_row)
        go(copy(udeg_part, udeg_recv.at[step], g_send.at[0, step], g_recv.at[0, step], row=peer))
    for step in range(1, n_col):
        peer = lax.rem(col + step, n_col)
        go(copy(qdeg_part, qdeg_recv.at[step], g_send.at[1, step], g_recv.at[1, step], col=peer))

    seed_count = seed_ids.shape[1]
    offset = (row * n_col + col) * q_local
    classes = groups * members
    class_hit = (
        lax.broadcasted_iota(jnp.int32, (classes, seed_count), 0) == seed_class[...]
    ).astype(jnp.float32).astype(jnp.bfloat16)
    place_hit = (
        lax.broadcasted_iota(jnp.int32, (q_local, seed_count), 0) == seed_ids[...] - offset
    ).astype(jnp.float32).astype(jnp.bfloat16)
    seeds[...] = (blend_rate * seed_weight) * lax.dot_general(
        class_hit, place_hit, across, preferred_element_type=jnp.float32
    )

    def finish_url_degrees():
        total = udeg_part[...]
        for step in range(1, n_row):
            copy(
                udeg_part, udeg_recv.at[step], g_send.at[0, step], g_recv.at[0, step],
                row=row,
            ).wait_recv()
            total = total + udeg_recv[step]
        inverse = 1.0 / (total + 1.0)
        for owner in range(n_row):
            udeg_inv[owner] = jnp.broadcast_to(inverse[owner:owner + 1, :], (8, u_local))

    def finish_query_degrees():
        total = qdeg_part[...]
        for step in range(1, n_col):
            copy(
                qdeg_part, qdeg_recv.at[step], g_send.at[1, step], g_recv.at[1, step],
                col=col,
            ).wait_recv()
            total = total + qdeg_recv[step]
        qdeg_inv[...] = (1.0 - blend_rate) / (total + 1.0)

    def flow(g):
        for it in range(ITERS):
            yield
            for step in range(1, n_col):
                copy(
                    qsend.at[it, g], place(qgrid[it][g], col, q_split, q_local),
                    a_send.at[it, g, step], a_recv.at[it, g, step], col=col,
                ).wait_recv()
            for k in range(slots):
                prods[k, 0:members, :] = jnp.dot(
                    qgrid[it][g][coords[0, k]], tiles[k], preferred_element_type=jnp.float32
                )
            for b in range(BC):
                total = combine(weight[b], lambda k: prods[k, 0:members, :])
                for i in range(u_split):
                    owner = b * u_split + i
                    part[it, g, owner % 2, owner // 2] = total[:, i * u_local:(i + 1) * u_local]
            go(copy(
                part.at[it, g, 1 - core], cross.at[it, g], b_send.at[it, g, 0], b_recv.at[it, g, 0],
                row=partner,
            ))
            yield
            copy(
                part.at[it, g, 1 - core], cross.at[it, g], b_send.at[it, g, 0], b_recv.at[it, g, 0],
                row=partner,
            ).wait_recv()
            if it == 0 and g == 0:
                finish_url_degrees()
            for step in list(range(1, chips)) + [0]:
                peer = lax.rem(chip + step, chips)
                both = part[it, g, core, peer] + cross[it, g, peer]
                both = both * udeg_inv[peer * 2 + core][0:1, :]
                if step == 0:
                    own[it, g] = both
                else:
                    encode(summed.at[it, g, step], both)
                    go(copy(
                        summed.at[it, g, step], rowbuf.at[it, g, step],
                        b_send.at[it, g, step], b_recv.at[it, g, step], row=peer * 2 + core,
                    ))
            yield
            total = own[it, g]
            for step in range(1, chips):
                copy(
                    summed.at[it, g, step], rowbuf.at[it, g, step],
                    b_send.at[it, g, step], b_recv.at[it, g, step], row=row,
                ).wait_recv()
                total = total + decode(rowbuf.at[it, g, step], u_local)
            url_labels = total
            if it == ITERS - 1:
                url_out[g * members:(g + 1) * members, :] = url_labels
            mine = place(ugrid[it][g], row, u_split, u_local)
            mine[...] = url_labels.astype(jnp.bfloat16)
            for step in range(1, chips):
                peer = lax.rem(chip + step, chips)
                go(copy(mine, mine, c_send.at[it, g, step], c_recv.at[it, g, step], row=peer * 2 + core))
            go(copy(mine, mine, c_send.at[it, g, 0], c_recv.at[it, g, 0], row=partner))
            yield
            for step in range(1, chips):
                source = lax.rem(chip + chips - step, chips) * 2 + core
                piece = place(ugrid[it][g], source, u_split, u_local)
                copy(piece, piece, c_send.at[it, g, step], c_recv.at[it, g, step], row=row).wait_recv()
                go(copy(
                    piece, piece, c_send.at[it, g, chips + step], c_recv.at[it, g, chips + step],
                    row=partner,
                ))
            if it == 0 and g == 0:
                finish_query_degrees()
            yield
            for step in range(chips):
                source = lax.rem(chip + chips - step, chips) * 2 + 1 - core
                piece = place(ugrid[it][g], source, u_split, u_local)
                index = chips + step if step else 0
                copy(piece, piece, c_send.at[it, g, index], c_recv.at[it, g, index], row=row).wait_recv()
            for k in range(slots):
                prods[k, 0:members, :] = lax.dot_general(
                    ugrid[it][g][coords[1, k]], tiles[k], across,
                    preferred_element_type=jnp.float32,
                )
            for a in range(q_blocks):
                total = combine(back_weight[a], lambda k: prods[k, 0:members, :])
                for i in range(q_split):
                    owner = a * q_split + i
                    scaled = total[:, i * q_local:(i + 1) * q_local] * qdeg_inv[owner:owner + 1, :]
                    dsend[it, g, owner] = scaled
            for step in range(1, n_col):
                peer = lax.rem(col + step, n_col)
                encode(dcode.at[it, g, step], dsend[it, g, peer])
                go(copy(
                    dcode.at[it, g, step], drecv.at[it, g, step],
                    d_send.at[it, g, step], d_recv.at[it, g, step], col=peer,
                ))
            yield
            total = dsend[it, g, col]
            for step in range(1, n_col):
                copy(
                    dcode.at[it, g, step], drecv.at[it, g, step],
                    d_send.at[it, g, step], d_recv.at[it, g, step], col=col,
                ).wait_recv()
                total = total + decode(drecv.at[it, g, step], q_local)
            rows = slice(g * members, (g + 1) * members)
            labels = total + seeds[rows, :]
            if it == ITERS - 1:
                labels_out[rows, :] = labels
            else:
                send_queries(it + 1, g, labels)
                start_queries(it + 1, g)
        yield

    flows = [flow(g) for g in range(groups)]
    for g in range(groups):
        next(flows[g])
    for it in range(ITERS):
        for stages in ((0,), (1,), (2,), (3, 4), (5,)):
            for g in range(groups):
                for stage in stages:
                    next(flows[g])
    for op in started:
        op.wait_send()


def shards(click_tiles, tile_coords, tile_count, prior_labels, seed_ids, seed_class):
    n_row, n_col = lax.axis_size("row"), lax.axis_size("col")
    slots, side = click_tiles.shape[0], click_tiles.shape[1]
    classes, q_local = prior_labels.shape
    q_blocks = q_local * n_col // side
    u_local = BC * side // n_row
    groups = GROUPS
    members = classes // groups
    chips = n_row // 2
    lead = (ITERS, groups)
    f32, bf16 = jnp.float32, jnp.bfloat16
    vmem = pl.BlockSpec(memory_space=pltpu.VMEM)
    scratch = [
        pltpu.VMEM((slots, side, side), bf16),
        pltpu.VMEM((slots, max(members, 16), side), f32),
        pltpu.VMEM(lead + (members, q_local), bf16),
        [[pltpu.VMEM((q_blocks, members, side), bf16)] * groups] * ITERS,
        pltpu.VMEM(lead + (2, chips, members, u_local), f32),
        pltpu.VMEM(lead + (chips, members, u_local), f32),
        pltpu.VMEM(lead + (chips, members, u_local + SCALE_LANES), jnp.int16),
        pltpu.VMEM(lead + (chips, members, u_local + SCALE_LANES), jnp.int16),
        pltpu.VMEM(lead + (members, u_local), f32),
        [[pltpu.VMEM((BC, members, side), bf16)] * groups] * ITERS,
        pltpu.VMEM(lead + (n_col, members, q_local), f32),
        pltpu.VMEM(lead + (n_col, members, q_local + SCALE_LANES), jnp.int16),
        pltpu.VMEM(lead + (n_col, members, q_local + SCALE_LANES), jnp.int16),
        pltpu.VMEM((n_row, u_local), f32),
        pltpu.VMEM((n_row, n_row, u_local), f32),
        pltpu.VMEM((max(n_col, 8), q_local), f32),
        pltpu.VMEM((n_col, max(n_col, 8), q_local), f32),
        pltpu.VMEM((n_row, 8, u_local), f32),
        pltpu.VMEM((max(n_col, 8), q_local), f32),
        pltpu.VMEM((classes, q_local), f32),
        pltpu.SMEM((2, slots), jnp.int32),
        pltpu.SMEM((1, 1), jnp.int32),
        pltpu.VMEM((classes, q_local), f32),
        pltpu.VMEM((1, seed_ids.shape[0]), jnp.int32),
        pltpu.VMEM((1, seed_ids.shape[0]), jnp.int32),
        pltpu.SemaphoreType.DMA((5,)),
        pltpu.SemaphoreType.DMA((slots,)),
        pltpu.SemaphoreType.DMA(lead + (n_col,)),
        pltpu.SemaphoreType.DMA(lead + (n_col,)),
        pltpu.SemaphoreType.DMA(lead + (chips,)),
        pltpu.SemaphoreType.DMA(lead + (chips,)),
        pltpu.SemaphoreType.DMA(lead + (2 * chips,)),
        pltpu.SemaphoreType.DMA(lead + (2 * chips,)),
        pltpu.SemaphoreType.DMA(lead + (n_col,)),
        pltpu.SemaphoreType.DMA(lead + (n_col,)),
        pltpu.SemaphoreType.DMA((2, max(n_row, n_col))),
        pltpu.SemaphoreType.DMA((2, max(n_row, n_col))),
    ]
    return pl.pallas_call(
        functools.partial(kernel, n_row, n_col),
        out_shape=(
            jax.ShapeDtypeStruct((classes, q_local), f32),
            jax.ShapeDtypeStruct((classes, u_local), f32),
        ),
        in_specs=[pl.BlockSpec(memory_space=pl.ANY)] * 6,
        out_specs=(vmem, vmem),
        scratch_shapes=scratch,
        compiler_params=pltpu.CompilerParams(
            collective_id=0, has_side_effects=True, vmem_limit_bytes=56 * 1024 * 1024
        ),
    )(tile_coords.T, tile_count[None, :], prior_labels, seed_ids[None, :], seed_class[None, :], click_tiles)


def solution(mesh):
    placed = (
        P(("row", "col"), None, None),
        P(("row", "col"), None),
        P(("row", "col")),
        P(None, ("row", "col")),
        P(("row", "col")),
        P(("row", "col")),
    )
    return jax.shard_map(
        shards,
        mesh=mesh,
        in_specs=placed,
        out_specs=(P(None, ("row", "col")), P(None, ("col", "row"))),
        check_vma=False,
    )
```

```python
import functools

import jax
import jax.numpy as jnp
from jax import lax
from jax.experimental import pallas as pl
from jax.experimental.pallas import tpu as pltpu
from jax.sharding import PartitionSpec as P

BC = 8
ITERS = 2
GROUPS = 4
WIRE_TOP = 32767.0
SCALE_LANES = 128
SCALE_STEPS = 256.0

blend_rate = 0.25
seed_weight = 8.0

MESH = pl.DeviceIdType.MESH


def encode(ref, values):
    top = jnp.maximum(jnp.max(values, axis=1, keepdims=True), 1e-30)
    power = jnp.floor(jnp.log2(top) * SCALE_STEPS) + 2.0
    steps = values * (WIRE_TOP * jnp.exp2(power * (-1.0 / SCALE_STEPS))) + 0.5
    width = values.shape[1]
    ref[:, 0:width] = steps.astype(jnp.int32).astype(jnp.int16)
    ref[:, width:width + SCALE_LANES] = jnp.broadcast_to(
        power, (values.shape[0], SCALE_LANES)
    ).astype(jnp.int32).astype(jnp.int16)


def decode(ref, width):
    power = ref[:, width:width + SCALE_LANES].astype(jnp.int32).astype(jnp.float32)
    unit = jnp.exp2(power * (1.0 / SCALE_STEPS)) * (1.0 / WIRE_TOP)
    return ref[:, 0:width].astype(jnp.int32).astype(jnp.float32) * unit[:, 0:1]


def kernel(
    n_row, n_col,
    coords_hbm, count_hbm, prior_hbm, seed_ids_hbm, seed_class_hbm, tiles_hbm,
    labels_out, url_out,
    tiles, prods, qsend, qgrid, part, cross, summed, rowbuf, own, ugrid, dsend, dcode, drecv,
    udeg_part, udeg_recv, qdeg_part, qdeg_recv, udeg_inv, qdeg_inv, seeds,
    coords, count, prior, seed_ids, seed_class, small_sem,
    tile_sem, a_send, a_recv, b_send, b_recv, c_send, c_recv, d_send, d_recv, g_send, g_recv,
):
    slots, side = tiles.shape[0], tiles.shape[1]
    groups, members = qsend.shape[1], qsend.shape[2]
    q_local, u_local = qsend.shape[3], url_out.shape[1]
    q_blocks = qgrid[0][0].shape[0]
    chips = n_row // 2
    q_split, u_split = side // q_local, side // u_local
    row, col = lax.axis_index("row"), lax.axis_index("col")
    chip, core = row // 2, row % 2
    partner = chip * 2 + 1 - core

    def place(ref, index, split, local):
        if split == 1:
            return ref.at[index]
        start = pl.multiple_of((index % split) * local, local)
        return ref.at[index // split, :, pl.ds(start, local)]

    def copy(src, dst, send, recv, **device):
        return pltpu.make_async_remote_copy(
            src_ref=src, dst_ref=dst, send_sem=send, recv_sem=recv,
            device_id=device, device_id_type=MESH,
        )

    started = []

    def go(op):
        op.start()
        started.append(op)

    small = [
        pltpu.make_async_copy(source, target, small_sem.at[i])
        for i, (source, target) in enumerate((
            (prior_hbm, prior), (coords_hbm, coords), (count_hbm, count),
            (seed_ids_hbm, seed_ids), (seed_class_hbm, seed_class),
        ))
    ]
    for load in small:
        load.start()
    loads = [
        pltpu.make_async_copy(tiles_hbm.at[k], tiles.at[k], tile_sem.at[k]) for k in range(slots)
    ]
    for load in loads:
        load.start()

    barrier = pltpu.get_barrier_semaphore()
    for step in range(1, n_row):
        pl.semaphore_signal(
            barrier, inc=1, device_id={"row": lax.rem(row + step, n_row)}, device_id_type=MESH
        )
    for step in range(1, n_col):
        pl.semaphore_signal(
            barrier, inc=1, device_id={"col": lax.rem(col + step, n_col)}, device_id_type=MESH
        )

    def send_queries(it, g, values):
        rounded = values.astype(jnp.bfloat16)
        qsend[it, g] = rounded
        here = place(qgrid[it][g], col, q_split, q_local)
        here[...] = rounded

    def start_queries(it, g):
        for step in range(1, n_col):
            go(copy(
                qsend.at[it, g], place(qgrid[it][g], col, q_split, q_local),
                a_send.at[it, g, step], a_recv.at[it, g, step],
                col=lax.rem(col + step, n_col),
            ))

    for load in small:
        load.wait()
    for g in range(groups):
        send_queries(0, g, prior[g * members:(g + 1) * members, :])
    pl.semaphore_wait(barrier, n_row + n_col - 2)
    for g in range(groups):
        start_queries(0, g)

    weight = [
        [
            jnp.where((coords[1, k] == b) & (k < count[0, 0]), 1.0, 0.0).astype(jnp.float32)
            for k in range(slots)
        ]
        for b in range(BC)
    ]
    back_weight = [
        [
            jnp.where((coords[0, k] == a) & (k < count[0, 0]), 1.0, 0.0).astype(jnp.float32)
            for k in range(slots)
        ]
        for a in range(q_blocks)
    ]

    def combine(weights, values):
        total = weights[0] * values(0)
        for k in range(1, slots):
            total = total + weights[k] * values(k)
        return total

    across = (((1,), (1,)), ((), ()))

    ones = jnp.ones((16, side), jnp.bfloat16)
    for k in range(slots):
        loads[k].wait()
        down = jnp.dot(ones, tiles[k], preferred_element_type=jnp.float32)
        along = lax.dot_general(ones, tiles[k], across, preferred_element_type=jnp.float32)
        prods[k, 0:8, :] = down[0:8]
        prods[k, 8:16, :] = along[0:8]
    for b in range(BC):
        total = combine(weight[b], lambda k: prods[k, 0:8, :])
        for i in range(u_split):
            udeg_part[pl.ds(b * u_split + i, 1), :] = total[0:1, i * u_local:(i + 1) * u_local]
    qdeg_part[...] = jnp.zeros_like(qdeg_part)
    for a in range(q_blocks):
        total = combine(back_weight[a], lambda k: prods[k, 8:16, :])
        for i in range(q_split):
            qdeg_part[pl.ds(a * q_split + i, 1), :] = total[0:1, i * q_local:(i + 1) * q_local]
    for step in range(1, n_row):
        peer = lax.rem(row + step, n_row)
        go(copy(udeg_part, udeg_recv.at[step], g_send.at[0, step], g_recv.at[0, step], row=peer))
    for step in range(1, n_col):
        peer = lax.rem(col + step, n_col)
        go(copy(qdeg_part, qdeg_recv.at[step], g_send.at[1, step], g_recv.at[1, step], col=peer))

    seed_count = seed_ids.shape[1]
    offset = (row * n_col + col) * q_local
    classes = groups * members
    class_hit = (
        lax.broadcasted_iota(jnp.int32, (classes, seed_count), 0) == seed_class[...]
    ).astype(jnp.float32).astype(jnp.bfloat16)
    place_hit = (
        lax.broadcasted_iota(jnp.int32, (q_local, seed_count), 0) == seed_ids[...] - offset
    ).astype(jnp.float32).astype(jnp.bfloat16)
    seeds[...] = (blend_rate * seed_weight) * lax.dot_general(
        class_hit, place_hit, across, preferred_element_type=jnp.float32
    )

    def finish_url_degrees():
        total = udeg_part[...]
        for step in range(1, n_row):
            copy(
                udeg_part, udeg_recv.at[step], g_send.at[0, step], g_recv.at[0, step],
                row=row,
            ).wait_recv()
            total = total + udeg_recv[step]
        inverse = 1.0 / (total + 1.0)
        for owner in range(n_row):
            udeg_inv[owner] = jnp.broadcast_to(inverse[owner:owner + 1, :], (8, u_local))

    def finish_query_degrees():
        total = qdeg_part[...]
        for step in range(1, n_col):
            copy(
                qdeg_part, qdeg_recv.at[step], g_send.at[1, step], g_recv.at[1, step],
                col=col,
            ).wait_recv()
            total = total + qdeg_recv[step]
        qdeg_inv[...] = (1.0 - blend_rate) / (total + 1.0)

    def flow(g):
        for it in range(ITERS):
            yield
            for step in range(1, n_col):
                copy(
                    qsend.at[it, g], place(qgrid[it][g], col, q_split, q_local),
                    a_send.at[it, g, step], a_recv.at[it, g, step], col=col,
                ).wait_recv()
            for k in range(slots):
                prods[k, 0:members, :] = jnp.dot(
                    qgrid[it][g][coords[0, k]], tiles[k], preferred_element_type=jnp.float32
                )
            for b in range(BC):
                total = combine(weight[b], lambda k: prods[k, 0:members, :])
                for i in range(u_split):
                    owner = b * u_split + i
                    part[it, g, owner % 2, owner // 2] = total[:, i * u_local:(i + 1) * u_local]
            go(copy(
                part.at[it, g, 1 - core], cross.at[it, g], b_send.at[it, g, 0], b_recv.at[it, g, 0],
                row=partner,
            ))
            yield
            copy(
                part.at[it, g, 1 - core], cross.at[it, g], b_send.at[it, g, 0], b_recv.at[it, g, 0],
                row=partner,
            ).wait_recv()
            if it == 0 and g == 0:
                finish_url_degrees()
            for step in list(range(1, chips)) + [0]:
                peer = lax.rem(chip + step, chips)
                both = part[it, g, core, peer] + cross[it, g, peer]
                both = both * udeg_inv[peer * 2 + core][0:1, :]
                if step == 0:
                    own[it, g] = both
                else:
                    encode(summed.at[it, g, step], both)
                    go(copy(
                        summed.at[it, g, step], rowbuf.at[it, g, step],
                        b_send.at[it, g, step], b_recv.at[it, g, step], row=peer * 2 + core,
                    ))
            yield
            total = own[it, g]
            for step in range(1, chips):
                copy(
                    summed.at[it, g, step], rowbuf.at[it, g, step],
                    b_send.at[it, g, step], b_recv.at[it, g, step], row=row,
                ).wait_recv()
                total = total + decode(rowbuf.at[it, g, step], u_local)
            url_labels = total
            if it == ITERS - 1:
                url_out[g * members:(g + 1) * members, :] = url_labels
            mine = place(ugrid[it][g], row, u_split, u_local)
            mine[...] = url_labels.astype(jnp.bfloat16)
            for step in range(1, chips):
                peer = lax.rem(chip + step, chips)
                go(copy(mine, mine, c_send.at[it, g, step], c_recv.at[it, g, step], row=peer * 2 + core))
            go(copy(mine, mine, c_send.at[it, g, 0], c_recv.at[it, g, 0], row=partner))
            yield
            for step in range(1, chips):
                source = lax.rem(chip + chips - step, chips) * 2 + core
                piece = place(ugrid[it][g], source, u_split, u_local)
                copy(piece, piece, c_send.at[it, g, step], c_recv.at[it, g, step], row=row).wait_recv()
                go(copy(
                    piece, piece, c_send.at[it, g, chips + step], c_recv.at[it, g, chips + step],
                    row=partner,
                ))
            if it == 0 and g == 0:
                finish_query_degrees()
            yield
            for step in range(chips):
                source = lax.rem(chip + chips - step, chips) * 2 + 1 - core
                piece = place(ugrid[it][g], source, u_split, u_local)
                index = chips + step if step else 0
                copy(piece, piece, c_send.at[it, g, index], c_recv.at[it, g, index], row=row).wait_recv()
            for k in range(slots):
                prods[k, 0:members, :] = lax.dot_general(
                    ugrid[it][g][coords[1, k]], tiles[k], across,
                    preferred_element_type=jnp.float32,
                )
            for a in range(q_blocks):
                total = combine(back_weight[a], lambda k: prods[k, 0:members, :])
                for i in range(q_split):
                    owner = a * q_split + i
                    scaled = total[:, i * q_local:(i + 1) * q_local] * qdeg_inv[owner:owner + 1, :]
                    dsend[it, g, owner] = scaled
            for step in range(1, n_col):
                peer = lax.rem(col + step, n_col)
                encode(dcode.at[it, g, step], dsend[it, g, peer])
                go(copy(
                    dcode.at[it, g, step], drecv.at[it, g, step],
                    d_send.at[it, g, step], d_recv.at[it, g, step], col=peer,
                ))
            yield
            total = dsend[it, g, col]
            for step in range(1, n_col):
                copy(
                    dcode.at[it, g, step], drecv.at[it, g, step],
                    d_send.at[it, g, step], d_recv.at[it, g, step], col=col,
                ).wait_recv()
                total = total + decode(drecv.at[it, g, step], q_local)
            rows = slice(g * members, (g + 1) * members)
            labels = total + seeds[rows, :]
            if it == ITERS - 1:
                labels_out[rows, :] = labels
            else:
                send_queries(it + 1, g, labels)
                start_queries(it + 1, g)
        yield

    stages = 6 * ITERS
    flows = [flow(g) for g in range(groups)]
    for g in range(groups):
        next(flows[g])
    for slot in range(stages + groups - 1):
        for g in range(groups):
            if 0 <= slot - g < stages:
                next(flows[g])
    for op in started:
        op.wait_send()


def shards(click_tiles, tile_coords, tile_count, prior_labels, seed_ids, seed_class):
    n_row, n_col = lax.axis_size("row"), lax.axis_size("col")
    slots, side = click_tiles.shape[0], click_tiles.shape[1]
    classes, q_local = prior_labels.shape
    q_blocks = q_local * n_col // side
    u_local = BC * side // n_row
    groups = GROUPS
    members = classes // groups
    chips = n_row // 2
    lead = (ITERS, groups)
    f32, bf16 = jnp.float32, jnp.bfloat16
    vmem = pl.BlockSpec(memory_space=pltpu.VMEM)
    scratch = [
        pltpu.VMEM((slots, side, side), bf16),
        pltpu.VMEM((slots, max(members, 16), side), f32),
        pltpu.VMEM(lead + (members, q_local), bf16),
        [[pltpu.VMEM((q_blocks, members, side), bf16)] * groups] * ITERS,
        pltpu.VMEM(lead + (2, chips, members, u_local), f32),
        pltpu.VMEM(lead + (chips, members, u_local), f32),
        pltpu.VMEM(lead + (chips, members, u_local + SCALE_LANES), jnp.int16),
        pltpu.VMEM(lead + (chips, members, u_local + SCALE_LANES), jnp.int16),
        pltpu.VMEM(lead + (members, u_local), f32),
        [[pltpu.VMEM((BC, members, side), bf16)] * groups] * ITERS,
        pltpu.VMEM(lead + (n_col, members, q_local), f32),
        pltpu.VMEM(lead + (n_col, members, q_local + SCALE_LANES), jnp.int16),
        pltpu.VMEM(lead + (n_col, members, q_local + SCALE_LANES), jnp.int16),
        pltpu.VMEM((n_row, u_local), f32),
        pltpu.VMEM((n_row, n_row, u_local), f32),
        pltpu.VMEM((max(n_col, 8), q_local), f32),
        pltpu.VMEM((n_col, max(n_col, 8), q_local), f32),
        pltpu.VMEM((n_row, 8, u_local), f32),
        pltpu.VMEM((max(n_col, 8), q_local), f32),
        pltpu.VMEM((classes, q_local), f32),
        pltpu.SMEM((2, slots), jnp.int32),
        pltpu.SMEM((1, 1), jnp.int32),
        pltpu.VMEM((classes, q_local), f32),
        pltpu.VMEM((1, seed_ids.shape[0]), jnp.int32),
        pltpu.VMEM((1, seed_ids.shape[0]), jnp.int32),
        pltpu.SemaphoreType.DMA((5,)),
        pltpu.SemaphoreType.DMA((slots,)),
        pltpu.SemaphoreType.DMA(lead + (n_col,)),
        pltpu.SemaphoreType.DMA(lead + (n_col,)),
        pltpu.SemaphoreType.DMA(lead + (chips,)),
        pltpu.SemaphoreType.DMA(lead + (chips,)),
        pltpu.SemaphoreType.DMA(lead + (2 * chips,)),
        pltpu.SemaphoreType.DMA(lead + (2 * chips,)),
        pltpu.SemaphoreType.DMA(lead + (n_col,)),
        pltpu.SemaphoreType.DMA(lead + (n_col,)),
        pltpu.SemaphoreType.DMA((2, max(n_row, n_col))),
        pltpu.SemaphoreType.DMA((2, max(n_row, n_col))),
    ]
    return pl.pallas_call(
        functools.partial(kernel, n_row, n_col),
        out_shape=(
            jax.ShapeDtypeStruct((classes, q_local), f32),
            jax.ShapeDtypeStruct((classes, u_local), f32),
        ),
        in_specs=[pl.BlockSpec(memory_space=pl.ANY)] * 6,
        out_specs=(vmem, vmem),
        scratch_shapes=scratch,
        compiler_params=pltpu.CompilerParams(
            collective_id=0, has_side_effects=True, vmem_limit_bytes=56 * 1024 * 1024
        ),
    )(tile_coords.T, tile_count[None, :], prior_labels, seed_ids[None, :], seed_class[None, :], click_tiles)


def solution(mesh):
    placed = (
        P(("row", "col"), None, None),
        P(("row", "col"), None),
        P(("row", "col")),
        P(None, ("row", "col")),
        P(("row", "col")),
        P(("row", "col")),
    )
    return jax.shard_map(
        shards,
        mesh=mesh,
        in_specs=placed,
        out_specs=(P(None, ("row", "col")), P(None, ("col", "row"))),
        check_vma=False,
    )
```

```python
import functools

import jax
import jax.numpy as jnp
from jax import lax
from jax.experimental import pallas as pl
from jax.experimental.pallas import tpu as pltpu
from jax.sharding import PartitionSpec as P

BC = 8
ITERS = 2
GROUPS = 1
WIRE_TOP = 32767.0
SCALE_LANES = 128
SCALE_STEPS = 256.0

blend_rate = 0.25
seed_weight = 8.0

MESH = pl.DeviceIdType.MESH


def encode(ref, values):
    top = jnp.maximum(jnp.max(values, axis=1, keepdims=True), 1e-30)
    power = jnp.floor(jnp.log2(top) * SCALE_STEPS) + 2.0
    steps = values * (WIRE_TOP * jnp.exp2(power * (-1.0 / SCALE_STEPS))) + 0.5
    width = values.shape[1]
    ref[:, 0:width] = steps.astype(jnp.int32).astype(jnp.int16)
    ref[:, width:width + SCALE_LANES] = jnp.broadcast_to(
        power, (values.shape[0], SCALE_LANES)
    ).astype(jnp.int32).astype(jnp.int16)


def decode(ref, width):
    power = ref[:, width:width + SCALE_LANES].astype(jnp.int32).astype(jnp.float32)
    unit = jnp.exp2(power * (1.0 / SCALE_STEPS)) * (1.0 / WIRE_TOP)
    return ref[:, 0:width].astype(jnp.int32).astype(jnp.float32) * unit[:, 0:1]


def kernel(
    n_row, n_col,
    coords_hbm, count_hbm, prior_hbm, seed_ids_hbm, seed_class_hbm, tiles_hbm,
    labels_out, url_out,
    tiles, prods, qsend, qgrid, part, cross, summed, rowbuf, own, ugrid, dsend, dcode, drecv,
    udeg_part, udeg_recv, qdeg_part, qdeg_recv, udeg_inv, qdeg_inv, seeds,
    coords, count, prior, seed_ids, seed_class, small_sem,
    tile_sem, a_send, a_recv, b_send, b_recv, c_send, c_recv, d_send, d_recv, g_send, g_recv,
):
    slots, side = tiles.shape[0], tiles.shape[1]
    groups, members = qsend.shape[1], qsend.shape[2]
    q_local, u_local = qsend.shape[3], url_out.shape[1]
    q_blocks = qgrid[0][0].shape[0]
    chips = n_row // 2
    q_split, u_split = side // q_local, side // u_local
    row, col = lax.axis_index("row"), lax.axis_index("col")
    chip, core = row // 2, row % 2
    partner = chip * 2 + 1 - core

    def place(ref, index, split, local):
        if split == 1:
            return ref.at[index]
        start = pl.multiple_of((index % split) * local, local)
        return ref.at[index // split, :, pl.ds(start, local)]

    def copy(src, dst, send, recv, **device):
        return pltpu.make_async_remote_copy(
            src_ref=src, dst_ref=dst, send_sem=send, recv_sem=recv,
            device_id=device, device_id_type=MESH,
        )

    started = []

    def go(op):
        op.start()
        started.append(op)

    small = [
        pltpu.make_async_copy(source, target, small_sem.at[i])
        for i, (source, target) in enumerate((
            (prior_hbm, prior), (coords_hbm, coords), (count_hbm, count),
            (seed_ids_hbm, seed_ids), (seed_class_hbm, seed_class),
        ))
    ]
    for load in small:
        load.start()
    loads = [
        pltpu.make_async_copy(tiles_hbm.at[k], tiles.at[k], tile_sem.at[k]) for k in range(slots)
    ]
    for load in loads:
        load.start()

    barrier = pltpu.get_barrier_semaphore()
    for step in range(1, n_row):
        pl.semaphore_signal(
            barrier, inc=1, device_id={"row": lax.rem(row + step, n_row)}, device_id_type=MESH
        )
    for step in range(1, n_col):
        pl.semaphore_signal(
            barrier, inc=1, device_id={"col": lax.rem(col + step, n_col)}, device_id_type=MESH
        )

    def send_queries(it, g, values):
        rounded = values.astype(jnp.bfloat16)
        qsend[it, g] = rounded
        here = place(qgrid[it][g], col, q_split, q_local)
        here[...] = rounded

    def start_queries(it, g):
        for step in range(1, n_col):
            go(copy(
                qsend.at[it, g], place(qgrid[it][g], col, q_split, q_local),
                a_send.at[it, g, step], a_recv.at[it, g, step],
                col=lax.rem(col + step, n_col),
            ))

    for load in small:
        load.wait()
    for g in range(groups):
        send_queries(0, g, prior[g * members:(g + 1) * members, :])
    pl.semaphore_wait(barrier, n_row + n_col - 2)
    for g in range(groups):
        start_queries(0, g)

    weight = [
        [
            jnp.where((coords[1, k] == b) & (k < count[0, 0]), 1.0, 0.0).astype(jnp.float32)
            for k in range(slots)
        ]
        for b in range(BC)
    ]
    back_weight = [
        [
            jnp.where((coords[0, k] == a) & (k < count[0, 0]), 1.0, 0.0).astype(jnp.float32)
            for k in range(slots)
        ]
        for a in range(q_blocks)
    ]

    def combine(weights, values):
        total = weights[0] * values(0)
        for k in range(1, slots):
            total = total + weights[k] * values(k)
        return total

    across = (((1,), (1,)), ((), ()))

    ones = jnp.ones((16, side), jnp.bfloat16)
    for k in range(slots):
        loads[k].wait()
        down = jnp.dot(ones, tiles[k], preferred_element_type=jnp.float32)
        along = lax.dot_general(ones, tiles[k], across, preferred_element_type=jnp.float32)
        prods[k, 0:8, :] = down[0:8]
        prods[k, 8:16, :] = along[0:8]
    for b in range(BC):
        total = combine(weight[b], lambda k: prods[k, 0:8, :])
        for i in range(u_split):
            udeg_part[pl.ds(b * u_split + i, 1), :] = total[0:1, i * u_local:(i + 1) * u_local]
    qdeg_part[...] = jnp.zeros_like(qdeg_part)
    for a in range(q_blocks):
        total = combine(back_weight[a], lambda k: prods[k, 8:16, :])
        for i in range(q_split):
            qdeg_part[pl.ds(a * q_split + i, 1), :] = total[0:1, i * q_local:(i + 1) * q_local]
    for step in range(1, n_row):
        peer = lax.rem(row + step, n_row)
        go(copy(udeg_part, udeg_recv.at[step], g_send.at[0, step], g_recv.at[0, step], row=peer))
    for step in range(1, n_col):
        peer = lax.rem(col + step, n_col)
        go(copy(qdeg_part, qdeg_recv.at[step], g_send.at[1, step], g_recv.at[1, step], col=peer))

    seed_count = seed_ids.shape[1]
    offset = (row * n_col + col) * q_local
    classes = groups * members
    class_hit = (
        lax.broadcasted_iota(jnp.int32, (classes, seed_count), 0) == seed_class[...]
    ).astype(jnp.float32).astype(jnp.bfloat16)
    place_hit = (
        lax.broadcasted_iota(jnp.int32, (q_local, seed_count), 0) == seed_ids[...] - offset
    ).astype(jnp.float32).astype(jnp.bfloat16)
    seeds[...] = (blend_rate * seed_weight) * lax.dot_general(
        class_hit, place_hit, across, preferred_element_type=jnp.float32
    )

    def finish_url_degrees():
        total = udeg_part[...]
        for step in range(1, n_row):
            copy(
                udeg_part, udeg_recv.at[step], g_send.at[0, step], g_recv.at[0, step],
                row=row,
            ).wait_recv()
            total = total + udeg_recv[step]
        inverse = 1.0 / (total + 1.0)
        for owner in range(n_row):
            udeg_inv[owner] = jnp.broadcast_to(inverse[owner:owner + 1, :], (8, u_local))

    def finish_query_degrees():
        total = qdeg_part[...]
        for step in range(1, n_col):
            copy(
                qdeg_part, qdeg_recv.at[step], g_send.at[1, step], g_recv.at[1, step],
                col=col,
            ).wait_recv()
            total = total + qdeg_recv[step]
        qdeg_inv[...] = (1.0 - blend_rate) / (total + 1.0)

    def flow(g):
        for it in range(ITERS):
            yield
            for step in range(1, n_col):
                copy(
                    qsend.at[it, g], place(qgrid[it][g], col, q_split, q_local),
                    a_send.at[it, g, step], a_recv.at[it, g, step], col=col,
                ).wait_recv()
            for k in range(slots):
                prods[k, 0:members, :] = jnp.dot(
                    qgrid[it][g][coords[0, k]], tiles[k], preferred_element_type=jnp.float32
                )
            for b in range(BC):
                total = combine(weight[b], lambda k: prods[k, 0:members, :])
                for i in range(u_split):
                    owner = b * u_split + i
                    part[it, g, owner % 2, owner // 2] = total[:, i * u_local:(i + 1) * u_local]
            go(copy(
                part.at[it, g, 1 - core], cross.at[it, g], b_send.at[it, g, 0], b_recv.at[it, g, 0],
                row=partner,
            ))
            yield
            copy(
                part.at[it, g, 1 - core], cross.at[it, g], b_send.at[it, g, 0], b_recv.at[it, g, 0],
                row=partner,
            ).wait_recv()
            if it == 0 and g == 0:
                finish_url_degrees()
            for step in list(range(1, chips)) + [0]:
                peer = lax.rem(chip + step, chips)
                both = part[it, g, core, peer] + cross[it, g, peer]
                both = both * udeg_inv[peer * 2 + core][0:1, :]
                if step == 0:
                    own[it, g] = both
                else:
                    encode(summed.at[it, g, step], both)
                    go(copy(
                        summed.at[it, g, step], rowbuf.at[it, g, step],
                        b_send.at[it, g, step], b_recv.at[it, g, step], row=peer * 2 + core,
                    ))
            yield
            total = own[it, g]
            for step in range(1, chips):
                copy(
                    summed.at[it, g, step], rowbuf.at[it, g, step],
                    b_send.at[it, g, step], b_recv.at[it, g, step], row=row,
                ).wait_recv()
                total = total + decode(rowbuf.at[it, g, step], u_local)
            url_labels = total
            if it == ITERS - 1:
                url_out[g * members:(g + 1) * members, :] = url_labels
            mine = place(ugrid[it][g], row, u_split, u_local)
            mine[...] = url_labels.astype(jnp.bfloat16)
            for step in range(1, chips):
                peer = lax.rem(chip + step, chips)
                go(copy(mine, mine, c_send.at[it, g, step], c_recv.at[it, g, step], row=peer * 2 + core))
            go(copy(mine, mine, c_send.at[it, g, 0], c_recv.at[it, g, 0], row=partner))
            yield
            for step in range(1, chips):
                source = lax.rem(chip + chips - step, chips) * 2 + core
                piece = place(ugrid[it][g], source, u_split, u_local)
                copy(piece, piece, c_send.at[it, g, step], c_recv.at[it, g, step], row=row).wait_recv()
                go(copy(
                    piece, piece, c_send.at[it, g, chips + step], c_recv.at[it, g, chips + step],
                    row=partner,
                ))
            if it == 0 and g == 0:
                finish_query_degrees()
            yield
            for step in range(chips):
                source = lax.rem(chip + chips - step, chips) * 2 + 1 - core
                piece = place(ugrid[it][g], source, u_split, u_local)
                index = chips + step if step else 0
                copy(piece, piece, c_send.at[it, g, index], c_recv.at[it, g, index], row=row).wait_recv()
            for k in range(slots):
                prods[k, 0:members, :] = lax.dot_general(
                    ugrid[it][g][coords[1, k]], tiles[k], across,
                    preferred_element_type=jnp.float32,
                )
            for a in range(q_blocks):
                total = combine(back_weight[a], lambda k: prods[k, 0:members, :])
                for i in range(q_split):
                    owner = a * q_split + i
                    scaled = total[:, i * q_local:(i + 1) * q_local] * qdeg_inv[owner:owner + 1, :]
                    dsend[it, g, owner] = scaled
            for step in range(1, n_col):
                peer = lax.rem(col + step, n_col)
                encode(dcode.at[it, g, step], dsend[it, g, peer])
                go(copy(
                    dcode.at[it, g, step], drecv.at[it, g, step],
                    d_send.at[it, g, step], d_recv.at[it, g, step], col=peer,
                ))
            yield
            total = dsend[it, g, col]
            for step in range(1, n_col):
                copy(
                    dcode.at[it, g, step], drecv.at[it, g, step],
                    d_send.at[it, g, step], d_recv.at[it, g, step], col=col,
                ).wait_recv()
                total = total + decode(drecv.at[it, g, step], q_local)
            rows = slice(g * members, (g + 1) * members)
            labels = total + seeds[rows, :]
            if it == ITERS - 1:
                labels_out[rows, :] = labels
            else:
                send_queries(it + 1, g, labels)
                start_queries(it + 1, g)
        yield

    flows = [flow(g) for g in range(groups)]
    for g in range(groups):
        next(flows[g])
    for it in range(ITERS):
        for stages in ((0,), (1,), (2,), (3, 4), (5,)):
            for g in range(groups):
                for stage in stages:
                    next(flows[g])
    for op in started:
        op.wait_send()


def shards(click_tiles, tile_coords, tile_count, prior_labels, seed_ids, seed_class):
    n_row, n_col = lax.axis_size("row"), lax.axis_size("col")
    slots, side = click_tiles.shape[0], click_tiles.shape[1]
    classes, q_local = prior_labels.shape
    q_blocks = q_local * n_col // side
    u_local = BC * side // n_row
    groups = GROUPS
    members = classes // groups
    chips = n_row // 2
    lead = (ITERS, groups)
    f32, bf16 = jnp.float32, jnp.bfloat16
    vmem = pl.BlockSpec(memory_space=pltpu.VMEM)
    scratch = [
        pltpu.VMEM((slots, side, side), bf16),
        pltpu.VMEM((slots, max(members, 16), side), f32),
        pltpu.VMEM(lead + (members, q_local), bf16),
        [[pltpu.VMEM((q_blocks, members, side), bf16)] * groups] * ITERS,
        pltpu.VMEM(lead + (2, chips, members, u_local), f32),
        pltpu.VMEM(lead + (chips, members, u_local), f32),
        pltpu.VMEM(lead + (chips, members, u_local + SCALE_LANES), jnp.int16),
        pltpu.VMEM(lead + (chips, members, u_local + SCALE_LANES), jnp.int16),
        pltpu.VMEM(lead + (members, u_local), f32),
        [[pltpu.VMEM((BC, members, side), bf16)] * groups] * ITERS,
        pltpu.VMEM(lead + (n_col, members, q_local), f32),
        pltpu.VMEM(lead + (n_col, members, q_local + SCALE_LANES), jnp.int16),
        pltpu.VMEM(lead + (n_col, members, q_local + SCALE_LANES), jnp.int16),
        pltpu.VMEM((n_row, u_local), f32),
        pltpu.VMEM((n_row, n_row, u_local), f32),
        pltpu.VMEM((max(n_col, 8), q_local), f32),
        pltpu.VMEM((n_col, max(n_col, 8), q_local), f32),
        pltpu.VMEM((n_row, 8, u_local), f32),
        pltpu.VMEM((max(n_col, 8), q_local), f32),
        pltpu.VMEM((classes, q_local), f32),
        pltpu.SMEM((2, slots), jnp.int32),
        pltpu.SMEM((1, 1), jnp.int32),
        pltpu.VMEM((classes, q_local), f32),
        pltpu.VMEM((1, seed_ids.shape[0]), jnp.int32),
        pltpu.VMEM((1, seed_ids.shape[0]), jnp.int32),
        pltpu.SemaphoreType.DMA((5,)),
        pltpu.SemaphoreType.DMA((slots,)),
        pltpu.SemaphoreType.DMA(lead + (n_col,)),
        pltpu.SemaphoreType.DMA(lead + (n_col,)),
        pltpu.SemaphoreType.DMA(lead + (chips,)),
        pltpu.SemaphoreType.DMA(lead + (chips,)),
        pltpu.SemaphoreType.DMA(lead + (2 * chips,)),
        pltpu.SemaphoreType.DMA(lead + (2 * chips,)),
        pltpu.SemaphoreType.DMA(lead + (n_col,)),
        pltpu.SemaphoreType.DMA(lead + (n_col,)),
        pltpu.SemaphoreType.DMA((2, max(n_row, n_col))),
        pltpu.SemaphoreType.DMA((2, max(n_row, n_col))),
    ]
    return pl.pallas_call(
        functools.partial(kernel, n_row, n_col),
        out_shape=(
            jax.ShapeDtypeStruct((classes, q_local), f32),
            jax.ShapeDtypeStruct((classes, u_local), f32),
        ),
        in_specs=[pl.BlockSpec(memory_space=pl.ANY)] * 6,
        out_specs=(vmem, vmem),
        scratch_shapes=scratch,
        compiler_params=pltpu.CompilerParams(
            collective_id=0, has_side_effects=True, vmem_limit_bytes=56 * 1024 * 1024
        ),
    )(tile_coords.T, tile_count[None, :], prior_labels, seed_ids[None, :], seed_class[None, :], click_tiles)


def solution(mesh):
    placed = (
        P(("row", "col"), None, None),
        P(("row", "col"), None),
        P(("row", "col")),
        P(None, ("row", "col")),
        P(("row", "col")),
        P(("row", "col")),
    )
    return jax.shard_map(
        shards,
        mesh=mesh,
        in_specs=placed,
        out_specs=(P(None, ("row", "col")), P(None, ("col", "row"))),
        check_vma=False,
    )
```
